256 devices in a mesh: segment: 4 (over x), dp: 64 (over y, z, core).
Axes of the slice: x: 4, y: 4, z: 8, core: 2. Of those that a mesh axis runs over, the one named last changes fastest.
Arguments:
- items: bfloat16 [32768, 3584], P(('segment', 'dp')), may hold values from -36 to 36
- section_weights: bfloat16 [4, 3584, 1792], P('segment', 'dp'), may hold values from -0.09375 to 0.09375
- section_gains: float32 [4, 3584], P('segment'), may hold values from 0.25 to 1.75
- student_gain: float32 [3584], replicated, may hold values from 0.25 to 1.75
- adapter: bfloat16 [3584, 1024], replicated, may hold values from -0.09375 to 0.09375
- out_gain: float32 [1024], replicated, may hold values from 0.25 to 1.75
- assign: int32 [32768, 2], P(('segment', 'dp')), may hold values from 0 to 255, all different within a row; in each aligned block of 128 rows (0 to 127, 128 to 255, ...) at most 2 rows name the same one
- teacher_scores: bfloat16 [32768, 2, 128], P(('segment', 'dp')), may hold values from -12 to 412
- bank: bfloat16 [65536, 1024], P(('segment', 'dp')), may hold values from -12 to 12
- bank_bias: float32 [65536], P(('segment', 'dp')), may hold values from -8 to 408
- neg_index: int32 [256, 128], P(('segment', 'dp')), may hold values from 0 to 255
Outputs:
- emb_grad: float32 [32768, 1024], P(('segment', 'dp'))
- row_kl: bfloat16 [32768, 2], P(('segment', 'dp'))
- bank_grad: float32 [65536, 1024], P(('segment', 'dp'))
The draws below stay inside these ranges and needn't reach their ends.
Inputs may be any that keep to these rules, and one draw needn't show every extreme that they name: `assign`: the 2 clusters of a row differ; among the rows of one device no cluster is named more than 2 times, and every cluster is named by some row.
All inputs are finite; a program needn't handle non-finite values.
Results may differ from the reference program's by a relative error of at most 0.035.
Values may be sent and summed in bfloat16 or wider, within the bound.
A program may use at most 128 MiB of HBM per device.

```python
import math
import jax
import jax.numpy as jnp
import numpy as np
from jax import lax

D_T = 3584
HD = 128
DS = 1024
NEG = 128
BANK_DEV = 256
TOPC = 2
ROWS_DEV = 128
H = 1792
ROWS = 32768
CLUSTERS = 256
CAP = 2
N_SEGMENT = 4
N_DP = 64


def draw_items(key, part):
    key = jax.random.fold_in(key, 11)
    base_key, column_key, row_key = jax.random.split(key, 3)
    columns = jnp.exp(jax.random.uniform(column_key, (1, D_T), jnp.float32, math.log(0.3), math.log(3.0)))
    row_scales = jnp.exp(jax.random.uniform(row_key, (ROWS, 1), jnp.float32, math.log(0.3), math.log(3.0)))
    values = jnp.clip(jax.random.normal(base_key, (ROWS, D_T), jnp.float32), -4.0, 4.0)
    return (values * columns * row_scales).astype(jnp.bfloat16)


def draw_teacher_scores(key, part):
    key = jax.random.fold_in(key, 12)
    base_key = jax.random.fold_in(key, 0)
    score_shape = (ROWS, TOPC, NEG)
    values = 3.0 * jnp.clip(jax.random.normal(base_key, score_shape, jnp.float32), -4.0, 4.0)
    return values.astype(jnp.bfloat16)


def draw_bank(key, part):
    key = jax.random.fold_in(key, 13)
    base_key, row_key = jax.random.split(key, 2)
    row_count = CLUSTERS * BANK_DEV
    row_scales = jnp.exp(jax.random.uniform(row_key, (row_count, 1), jnp.float32, math.log(0.3), math.log(3.0)))
    values = jnp.clip(jax.random.normal(base_key, (row_count, DS), jnp.float32), -4.0, 4.0)
    return (values * row_scales).astype(jnp.bfloat16)


def draw_bank_bias(key, part):
    key = jax.random.fold_in(key, 14)
    base_key = jax.random.fold_in(key, 0)
    row_count = CLUSTERS * BANK_DEV
    values = 2.0 * jnp.clip(jax.random.normal(base_key, (row_count,), jnp.float32), -4.0, 4.0)
    return values.astype(jnp.float32)


def set_ends(drawn, rng, least, high):
    dims = drawn.shape
    index_at = [jax.random.randint(jax.random.fold_in(rng, axis), (), 0, dims[axis]) for axis in range(len(dims))]
    drawn = drawn.at[tuple(index_at)].set(least)
    longest = dims.index(max(dims))
    index_at[longest] = (index_at[longest] + 1) % dims[longest]
    return drawn.at[tuple(index_at)].set(high)


def block_levels(own_key, shape, pieces, smallest, largest):
    loudness = 1.0
    for dim, blocks in pieces:
        steps = jax.random.uniform(jax.random.fold_in(jax.random.fold_in(own_key, 6), dim), (blocks,), jnp.float32, smallest / len(pieces), largest / len(pieces))
        loudness = loudness * jnp.repeat(jnp.exp(steps), shape[dim] // blocks).reshape((-1,) + (1,) * (len(shape) - 1 - dim))
    return loudness


def deal_out(key, own, number, rows, count, top, most, slope):
    order = jax.random.permutation(key, count)
    heavy_load, common = portions_of(count, rows * top, most, slope, True), portions_of(count, rows * top, most, slope, False)
    places = jnp.arange(count)

    def named(tallies, turn):
        used = int((tallies > 0).sum())
        fixed = max(1, used // 4)
        shifted = fixed + (places - fixed + turn * (used - fixed)) % max(1, count - fixed)
        return jnp.zeros((count,), jnp.int32).at[order[jnp.where(places < fixed, places, shifted)]].set(jnp.asarray(tallies, jnp.int32))

    tallies = jnp.where(number % 4 == 0, named(heavy_load, number // 4), named(common, number - number // 4 - 1))
    mixed = jax.random.permutation(jax.random.fold_in(own, 3), count)
    giver, taker = mixed[0:count // 2 * 2:2], mixed[1:count // 2 * 2:2]
    room = jnp.minimum(tallies[giver] - 1, most - tallies[taker]) // 2
    room = jnp.where((giver == order[0]) | (taker == order[0]) | (tallies[taker] == 0), 0, jnp.maximum(room, 0))
    shifted = jax.random.randint(jax.random.fold_in(own, 4), (count // 2,), 0, 1 << 20) % (room + 1)
    tallies = tallies.at[giver].add(-shifted).at[taker].add(shifted)
    members = jnp.searchsorted(jnp.cumsum(tallies), jnp.arange(rows * top), side="right").astype(jnp.int32)
    listing = members.reshape(top, rows).T
    listing = listing[jax.random.permutation(jax.random.fold_in(own, 1), rows)]
    turn = jax.random.randint(jax.random.fold_in(own, 2), (rows, 1), 0, top)
    return jnp.take_along_axis(listing, (jnp.arange(top)[None, :] + turn) % top, axis=1)


def portions_of(amount, total, reach, lean, full):
    portions = [(1 << 20) // math.isqrt(grade ** lean) + 1 for grade in range(1, amount + 1)]
    largest = reach if full else min(reach, max(-(-total // amount), total * portions[0] // sum(portions)))
    least = 1 if total - largest >= amount - 1 else 0
    holding, surplus = [largest] + [least] * (amount - 1), total - largest - least * (amount - 1)
    while surplus > 0:
        movable = [i for i in range(1, amount) if holding[i] < largest] or [i for i in range(1, amount) if holding[i] < reach]
        mass, remaining = sum([portions[i] for i in movable]), surplus
        for i in movable:
            more = min(reach - holding[i], max(1, remaining * portions[i] // mass), surplus)
            holding[i] = holding[i] + more
            surplus = surplus - more
    return np.array(holding)


def noise(rng, shape, width, reach, shards=(), kind=jnp.bfloat16):
    level = block_levels(rng, shape, shards, -0.22, 0.18) if shards else 1.0
    values = jax.random.normal(rng, shape, jnp.float32) * width * level
    return jnp.minimum(jnp.maximum(values, -reach), reach).astype(kind)


def setup_inputs(seed: int = 0) -> dict:
    seeds = jax.random.split(jax.random.key(seed), 12)
    items = draw_items(jax.random.fold_in(seeds[11], 71), 0)
    section_weights = noise(seeds[1], (N_SEGMENT, D_T, H), D_T ** -0.5, 0.09375, ((0, 4), (1, 64)))
    section_gains = jnp.clip(1.0 + 0.15 * jax.random.normal(seeds[2], (N_SEGMENT, D_T), jnp.float32), 0.25, 1.75)
    student_gain = jnp.clip(1.0 + 0.15 * jax.random.normal(seeds[3], (D_T,), jnp.float32), 0.25, 1.75)
    adapter = noise(seeds[4], (D_T, DS), D_T ** -0.5, 0.09375)
    out_gain = jnp.clip(1.0 + 0.15 * jax.random.normal(seeds[5], (DS,), jnp.float32), 0.25, 1.75)
    assign_keys = jax.random.split(jax.random.fold_in(seeds[6], 1), ROWS // ROWS_DEV)
    assign_turns = jax.random.permutation(jax.random.fold_in(seeds[6], 3), ROWS // ROWS_DEV)
    assign = jax.vmap(lambda own, number: deal_out(jax.random.fold_in(seeds[6], 2), own, number, ROWS_DEV, CLUSTERS, TOPC, CAP, 2))(assign_keys, assign_turns).reshape((ROWS, TOPC))
    teacher_scores = draw_teacher_scores(jax.random.fold_in(seeds[11], 71), 0)
    bank = draw_bank(jax.random.fold_in(seeds[11], 71), 0)
    bank_bias = draw_bank_bias(jax.random.fold_in(seeds[11], 71), 0)
    neg_index = set_ends(jax.random.randint(seeds[10], (CLUSTERS, NEG), 0, BANK_DEV), jax.random.fold_in(seeds[10], 1), 0, BANK_DEV - 1).astype(jnp.int32)
    return dict(items=items, section_weights=section_weights, section_gains=section_gains, student_gain=student_gain, adapter=adapter, out_gain=out_gain, assign=assign, teacher_scores=teacher_scores, bank=bank, bank_bias=bank_bias, neg_index=neg_index)


eps = 1e-06
temper = 4.0

def normalize(values, scale_row):
    values = values.astype(jnp.float32)
    return values * lax.rsqrt(lax.optimization_barrier(jnp.mean(values * values, axis=-1, keepdims=True)) + eps) * scale_row

def head_normalize(values):
    count = values.shape[0]
    head_values = values.astype(jnp.float32).reshape(count, values.shape[1] // HD, HD)
    head_values = head_values * lax.rsqrt(lax.optimization_barrier(jnp.mean(head_values * head_values, axis=-1, keepdims=True)) + eps)
    return head_values.reshape(count, values.shape[1]).astype(jnp.bfloat16)

def embed_block(block, section_weights, section_gains, student_gain, adapter, out_gain):
    carried = block
    for section in range(N_SEGMENT):
        if section % 2 == 0:
            normed = normalize(carried, section_gains[section]).astype(jnp.bfloat16)
            carried = jnp.dot(normed, section_weights[section], preferred_element_type=jnp.float32).astype(jnp.bfloat16)
        else:
            normed = head_normalize(carried)
            projected = jnp.dot(normed, section_weights[section].T, preferred_element_type=jnp.float32)
            carried = (projected * section_gains[section]).astype(jnp.bfloat16)
    normed = normalize(carried, student_gain).astype(jnp.bfloat16)
    raw_embed = jnp.dot(normed, adapter, preferred_element_type=jnp.float32)
    return normalize(raw_embed, out_gain).astype(jnp.bfloat16)

def cluster_block(slot_embed, slot_scores, slot_valid, bank_block, bias_block, neg_rows):
    negatives = jnp.take(bank_block, neg_rows, axis=0)
    offsets = jnp.take(bias_block, neg_rows, axis=0)
    score_scale = temper * DS ** (-0.5)
    logits = jnp.dot(slot_embed, negatives.T, preferred_element_type=jnp.float32) * score_scale + offsets
    student_log = jax.nn.log_softmax(logits, axis=-1)
    teacher_log = jax.nn.log_softmax(slot_scores.astype(jnp.float32), axis=-1)
    teacher_prob = jnp.exp(teacher_log)
    divergence = lax.optimization_barrier(jnp.sum(teacher_prob * (teacher_log - student_log), axis=-1)).astype(jnp.bfloat16)
    prob_gap = (slot_valid[:, None] * (jnp.exp(student_log) - teacher_prob)).astype(jnp.bfloat16)
    slot_grad = (jnp.dot(prob_gap, negatives, preferred_element_type=jnp.float32) * score_scale).astype(jnp.bfloat16)
    neg_grad = jnp.dot(prob_gap.T, slot_embed, preferred_element_type=jnp.float32) * score_scale
    bank_grad = jnp.zeros(bank_block.shape, jnp.float32).at[neg_rows].add(neg_grad)
    return (slot_grad, divergence, bank_grad)

def reference(items, section_weights, section_gains, student_gain, adapter, out_gain, assign, teacher_scores, bank, bank_bias, neg_index):
    devices_all = N_SEGMENT * N_DP
    blocks = items.reshape(devices_all, ROWS_DEV, D_T)
    embeds = lax.map(lambda block: embed_block(block, section_weights, section_gains, student_gain, adapter, out_gain), blocks)
    pair_count = ROWS_DEV * TOPC
    pair_cluster = assign.reshape(devices_all, pair_count).astype(jnp.int32)
    member = (pair_cluster[:, :, None] == jnp.arange(CLUSTERS, dtype=jnp.int32)[None, None, :]).astype(jnp.int32)
    pair_rank = lax.optimization_barrier(jnp.sum(jnp.cumsum(member, axis=1) * member, axis=2)) - 1
    source = jnp.arange(devices_all, dtype=jnp.int32)[:, None]
    slot_index = (source * CAP + pair_rank).astype(jnp.int32)
    slot_total = devices_all * CAP
    pair_embed = jnp.repeat(embeds, TOPC, axis=1)
    slot_embed = jnp.zeros((CLUSTERS, slot_total, DS), jnp.bfloat16).at[pair_cluster, slot_index].set(pair_embed)
    pair_scores = teacher_scores.reshape(devices_all, pair_count, NEG)
    slot_scores = jnp.zeros((CLUSTERS, slot_total, NEG), jnp.bfloat16).at[pair_cluster, slot_index].set(pair_scores)
    slot_valid = jnp.zeros((CLUSTERS, slot_total), jnp.float32).at[pair_cluster, slot_index].set(1.0)
    slot_grad, divergence, bank_grad = lax.map(lambda parts: cluster_block(parts[0], parts[1], parts[2], parts[3], parts[4], parts[5]), (slot_embed, slot_scores, slot_valid, bank.reshape(CLUSTERS, BANK_DEV, DS), bank_bias.reshape(CLUSTERS, BANK_DEV), neg_index.astype(jnp.int32)))
    pair_grad = slot_grad[pair_cluster, slot_index].astype(jnp.float32).reshape(ROWS_DEV * devices_all, TOPC, DS)
    emb_grad = lax.optimization_barrier(jnp.sum(pair_grad, axis=1))
    row_kl = divergence[pair_cluster, slot_index].reshape(ROWS_DEV * devices_all, TOPC)
    return (emb_grad, row_kl, bank_grad.reshape(CLUSTERS * BANK_DEV, DS))
```

```python
import functools

import jax
import jax.numpy as jnp
from jax import lax
from jax.experimental import pallas as pl
from jax.experimental.pallas import tpu as pltpu
from jax.sharding import PartitionSpec as P

HD = 128
MESH = pl.DeviceIdType.MESH

eps = 1e-06
temper = 4.0

SIZES = (4, 4, 8)
ORDERS = ((0, 1, 2), (1, 2, 0), (2, 0, 1))
PART_HEADS = (4, 5, 5)


def normalize(values, scale_row):
    values = values.astype(jnp.float32)
    return values * lax.rsqrt(jnp.mean(values * values, axis=-1, keepdims=True) + eps) * scale_row


def ring_plan():
    ready = {}
    hops = []
    free = {}
    todo = []
    for part, order in enumerate(ORDERS):
        for phase, axis in enumerate(order):
            for long_way in (True, False):
                steps = SIZES[axis] // 2 - (0 if long_way else 1)
                for step in range(steps):
                    todo.append((part, phase, long_way, step))
    blocks = lambda part, phase: PART_HEADS[part] * (
        1
        if phase == 0
        else SIZES[ORDERS[part][0]] * (1 if phase == 1 else SIZES[ORDERS[part][1]])
    )
    done = {}

    def start_of(hop):
        part, phase, long_way, step = hop
        if step > 0:
            return done.get((part, phase, long_way, step - 1))
        if phase == 0:
            return 0.0
        before = [h for h in todo_all if h[0] == part and h[1] == phase - 1]
        if any(h not in done for h in before):
            return None
        return max(done[h] for h in before)

    todo_all = list(todo)
    while todo:
        options = []
        for hop in todo:
            start = start_of(hop)
            if start is not None:
                axis = ORDERS[hop[0]][hop[1]]
                link = (axis, hop[2])
                options.append((max(start, free.get(link, 0.0)), hop, link))
        start, hop, link = min(options)
        share = 1.5 if hop[2] else 1.5
        finish = start + share * blocks(hop[0], hop[1]) + 1.0
        done[hop] = finish
        free[link] = start + share * blocks(hop[0], hop[1])
        todo.remove(hop)
        hops.append(hop)
    return sorted(hops, key=lambda hop: done[hop])


def gather_kernel(w_ref, out_ref, local_sem, send_sem, recv_sem, sib_send, sib_recv):
    x = lax.axis_index("segment")
    dp = lax.axis_index("dp")
    core = dp % 2
    z = (dp // 2) % SIZES[2]
    y = dp // (2 * SIZES[2])
    here = (x, y, z)

    def device(at, on):
        return (at[0], (at[1] * SIZES[2] + at[2]) * 2 + on)

    def moved(axis, by):
        at = list(here)
        at[axis] = (here[axis] + by + 2 * SIZES[axis]) % SIZES[axis]
        return tuple(at)

    sign = 1 - 2 * core
    sibling = device(here, 1 - core)

    mine = out_ref.at[x, y, z, core]
    own = pltpu.make_async_copy(w_ref, mine, local_sem)
    own.start()

    barrier = pltpu.get_barrier_semaphore()
    partners = [device(moved(axis, by), core) for axis in range(3) for by in (1, -1)] + [sibling]
    for partner in partners:
        pl.semaphore_signal(barrier, inc=1, device_id=partner, device_id_type=MESH)
    pl.semaphore_wait(barrier, len(partners))
    own.wait()

    starts = [sum(PART_HEADS[:part]) * HD for part in range(3)]

    def block(part, phase, place, on=core):
        order = ORDERS[part]
        at = list(here)
        at[order[phase]] = place
        for earlier in order[:phase]:
            at[earlier] = slice(None)
        return out_ref.at[
            at[0], at[1], at[2], on, :, pl.ds(starts[part], PART_HEADS[part] * HD)
        ]

    plan = ring_plan()
    number = {hop: i for i, hop in enumerate(plan)}
    sends = []

    def hop_copy(hop, sending):
        part, phase, long_way, step = hop
        axis = ORDERS[part][phase]
        size = SIZES[axis]
        toward = sign if long_way else -sign
        behind = step if sending else step + 1
        place = (here[axis] - toward * behind + 2 * size) % size
        held = block(part, phase, place)
        return pltpu.make_async_remote_copy(
            src_ref=held,
            dst_ref=held,
            send_sem=send_sem.at[number[hop]],
            recv_sem=recv_sem.at[number[hop]],
            device_id=device(moved(axis, toward), core),
            device_id_type=MESH,
        )

    def start(hop):
        copy = hop_copy(hop, True)
        copy.start()
        sends.append(copy)

    def to_sibling(index, held):
        copy = pltpu.make_async_remote_copy(
            src_ref=held,
            dst_ref=held,
            send_sem=sib_send.at[index],
            recv_sem=sib_recv.at[index],
            device_id=sibling,
            device_id_type=MESH,
        )
        copy.start()
        sends.append(copy)

    started = set()
    arrived = set()

    def start_ready():
        for hop in plan:
            if hop in started:
                continue
            part, phase, long_way, step = hop
            if step > 0:
                ready = (part, phase, long_way, step - 1) in arrived
            elif phase == 0:
                ready = True
            else:
                ready = all(h in arrived for h in plan if h[0] == part and h[1] == phase - 1)
            if ready:
                start(hop)
                started.add(hop)

    start_ready()
    to_sibling(len(plan), mine)
    for hop in plan:
        hop_copy(hop, False).wait_recv()
        arrived.add(hop)
        start_ready()
        part, phase, long_way, step = hop
        axis = ORDERS[part][phase]
        toward = sign if long_way else -sign
        place = (here[axis] - toward * (step + 1) + 2 * SIZES[axis]) % SIZES[axis]
        to_sibling(number[hop], block(part, phase, place))

    other = 1 - core
    for hop in plan:
        part, phase, long_way, step = hop
        axis = ORDERS[part][phase]
        toward = -sign if long_way else sign
        place = (here[axis] - toward * (step + 1) + 2 * SIZES[axis]) % SIZES[axis]
        held = block(part, phase, place, other)
        pltpu.make_async_remote_copy(
            src_ref=held,
            dst_ref=held,
            send_sem=sib_send.at[number[hop]],
            recv_sem=sib_recv.at[number[hop]],
            device_id=sibling,
            device_id_type=MESH,
        ).wait_recv()
    theirs = out_ref.at[x, y, z, other]
    pltpu.make_async_remote_copy(
        src_ref=theirs,
        dst_ref=theirs,
        send_sem=sib_send.at[len(plan)],
        recv_sem=sib_recv.at[len(plan)],
        device_id=sibling,
        device_id_type=MESH,
    ).wait_recv()
    for copy in sends:
        copy.wait_send()


def gather_weights(shard):
    rows, width = shard.shape
    hops = len(ring_plan())
    return pl.pallas_call(
        gather_kernel,
        out_shape=jax.ShapeDtypeStruct((*SIZES, 2, rows, width), shard.dtype),
        in_specs=[pl.BlockSpec(memory_space=pl.ANY)],
        out_specs=pl.BlockSpec(memory_space=pl.ANY),
        scratch_shapes=[
            pltpu.SemaphoreType.DMA,
            pltpu.SemaphoreType.DMA((hops,)),
            pltpu.SemaphoreType.DMA((hops,)),
            pltpu.SemaphoreType.DMA((hops + 1,)),
            pltpu.SemaphoreType.DMA((hops + 1,)),
        ],
        compiler_params=pltpu.CompilerParams(collective_id=0, has_side_effects=True),
        name="gather_weights",
    )(shard)


def value_section(carried, weight, scale_row):
    normed = normalize(carried, scale_row).astype(jnp.bfloat16)
    return jnp.dot(normed, weight, preferred_element_type=jnp.float32).astype(jnp.bfloat16)


def output_section(carried, weight, scale_row):
    rows, width = carried.shape
    heads = carried.astype(jnp.float32).reshape(rows, width // HD, HD)
    heads = heads * lax.rsqrt(jnp.mean(heads * heads, axis=-1, keepdims=True) + eps)
    normed = heads.reshape(rows, width).astype(jnp.bfloat16)
    projected = lax.dot_general(
        normed, weight, (((1,), (1,)), ((), ())), preferred_element_type=jnp.float32
    )
    return (projected * scale_row).astype(jnp.bfloat16)


def student(teacher_out, student_gain, adapter, out_gain):
    normed = normalize(teacher_out, student_gain).astype(jnp.bfloat16)
    raw_embed = jnp.dot(normed, adapter, preferred_element_type=jnp.float32)
    return normalize(raw_embed, out_gain).astype(jnp.bfloat16)


def shards(
    items,
    section_weights,
    section_gains,
    student_gain,
    adapter,
    out_gain,
    assign,
    teacher_scores,
    bank,
    bank_bias,
    neg_index,
):
    segments = lax.axis_size("segment")
    dp_count = lax.axis_size("dp")
    both = ("segment", "dp")
    owners = segments * dp_count

    gathered = gather_weights(section_weights[0])
    weights = gathered.reshape(segments, -1, section_weights.shape[2])
    gains = lax.all_gather(section_gains[0], "segment", axis=0)
    carried = items
    for section in range(segments):
        run = output_section if section % 2 else value_section
        carried = run(carried, weights[section], gains[section])
    embedding = student(carried, student_gain, adapter, out_gain)

    row_count = embedding.shape[0]
    pick_count = assign.shape[1]
    pair_count = row_count * pick_count
    capacity = max(2, 2 * pair_count // owners)
    slot_count = owners * capacity
    pair_cluster = assign.reshape(-1)
    same = pair_cluster[:, None] == pair_cluster[None, :]
    earlier = jnp.arange(pair_count)[:, None] > jnp.arange(pair_count)[None, :]
    pair_rank = jnp.sum((same & earlier).astype(jnp.int32), axis=1)
    target = pair_cluster * capacity + pair_rank
    pick_map = target[None, :] == jnp.arange(slot_count, dtype=jnp.int32)[:, None]
    pair_map = pick_map.astype(jnp.bfloat16)
    row_map = jnp.any(pick_map.reshape(slot_count, row_count, pick_count), axis=2).astype(
        jnp.bfloat16
    )
    sent_embed = jnp.dot(row_map, embedding, preferred_element_type=jnp.float32).astype(
        jnp.bfloat16
    )
    scores = teacher_scores.reshape(pair_count, -1)
    sent_scores = jnp.dot(pair_map, scores, preferred_element_type=jnp.float32).astype(jnp.bfloat16)
    valid = jnp.broadcast_to(
        jnp.sum(pick_map.astype(jnp.float32), axis=1, keepdims=True).astype(jnp.bfloat16),
        sent_scores.shape,
    )
    side = jnp.concatenate([sent_scores, valid], axis=1)

    def exchange(block):
        width = block.shape[1]
        block = block.reshape(owners, capacity * width)
        block = lax.all_to_all(block, both, split_axis=0, concat_axis=0, tiled=True)
        return block.reshape(slot_count, width)

    got_side = exchange(side)
    slot_embed = exchange(sent_embed)
    slot_scores = got_side[:, : scores.shape[1]].astype(jnp.float32)
    slot_valid = got_side[:, scores.shape[1]].astype(jnp.float32)

    neg_rows = neg_index[0]
    pool_size = bank.shape[0]
    embed_width = bank.shape[1]
    choose = neg_rows[:, None] == jnp.arange(pool_size, dtype=jnp.int32)[None, :]
    negatives = jnp.dot(
        choose.astype(jnp.bfloat16), bank, preferred_element_type=jnp.float32
    ).astype(jnp.bfloat16)
    offsets = jnp.dot(choose.astype(jnp.float32), bank_bias, precision=lax.Precision.HIGHEST)
    score_scale = temper * embed_width ** (-0.5)
    logits = (
        lax.dot_general(
            slot_embed, negatives, (((1,), (1,)), ((), ())), preferred_element_type=jnp.float32
        )
        * score_scale
        + offsets
    )
    student_log = jax.nn.log_softmax(logits, axis=-1)
    teacher_log = jax.nn.log_softmax(slot_scores, axis=-1)
    teacher_prob = jnp.exp(teacher_log)
    divergence = jnp.sum(teacher_prob * (teacher_log - student_log), axis=-1).astype(jnp.bfloat16)
    prob_gap = (slot_valid[:, None] * (jnp.exp(student_log) - teacher_prob)).astype(jnp.bfloat16)
    slot_grad = (
        jnp.dot(prob_gap, negatives, preferred_element_type=jnp.float32) * score_scale
    ).astype(jnp.bfloat16)
    neg_grad = (
        lax.dot_general(
            prob_gap, slot_embed, (((0,), (0,)), ((), ())), preferred_element_type=jnp.float32
        )
        * score_scale
    )
    bank_grad = lax.dot_general(
        choose.astype(jnp.float32),
        neg_grad,
        (((0,), (0,)), ((), ())),
        precision=lax.Precision.HIGHEST,
    )
    home_grad = exchange(slot_grad)
    home_kl = exchange(jnp.broadcast_to(divergence[:, None], (slot_count, HD)))[:, :1]
    emb_grad = lax.dot_general(
        row_map, home_grad, (((0,), (0,)), ((), ())), preferred_element_type=jnp.float32
    )
    row_kl = lax.dot_general(
        pair_map, home_kl, (((0,), (0,)), ((), ())), preferred_element_type=jnp.float32
    )
    row_kl = row_kl.astype(jnp.bfloat16).reshape(row_count, pick_count)
    return (emb_grad, row_kl, bank_grad)


def solution(mesh):
    in_specs = (
        P(("segment", "dp"), None),
        P("segment", "dp", None),
        P("segment", None),
        P(),
        P(),
        P(),
        P(("segment", "dp"), None),
        P(("segment", "dp"), None, None),
        P(("segment", "dp"), None),
        P(("segment", "dp")),
        P(("segment", "dp"), None),
    )
    out_specs = (P(("segment", "dp"), None), P(("segment", "dp"), None), P(("segment", "dp"), None))
    return jax.shard_map(shards, mesh=mesh, in_specs=in_specs, out_specs=out_specs, check_vma=False)
```

```python
import functools

import jax
import jax.numpy as jnp
from jax import lax
from jax.experimental import pallas as pl
from jax.experimental.pallas import tpu as pltpu
from jax.sharding import PartitionSpec as P

HD = 128
MESH = pl.DeviceIdType.MESH
F32 = jnp.float32
BF16 = jnp.bfloat16

eps = 1e-06
temper = 4.0
UNUSED = -1e30

SIZES = (4, 4, 8)
ORDERS = ((0, 1, 2), (2, 1, 0), (0, 2, 1))
PART_ROWS = (32, 48, 32)


def dot(a, b, contract=((1,), (0,))):
    return lax.dot_general(a, b, (contract, ((), ())), preferred_element_type=F32)


def normalize(values, scale_row):
    return values * lax.rsqrt(jnp.mean(values * values, axis=-1, keepdims=True) + eps) * scale_row


def offsets_along(size):
    return [0] + list(range(1, size // 2 + 1)) + [-k for k in range(1, size // 2)]


def gather_plan(latency=25.0):
    rows = {}
    for part, order in enumerate(ORDERS):
        for phase, axis in enumerate(order):
            if phase == 0:
                subs = [()]
            elif phase == 1:
                subs = [(k,) for k in offsets_along(SIZES[order[0]])]
            else:
                subs = [(None, k) for k in offsets_along(SIZES[order[1]])]
            for sub in subs:
                count = PART_ROWS[part] * (SIZES[order[0]] if phase == 2 else 1)
                for k in offsets_along(SIZES[axis]):
                    if k:
                        rows[part, phase, k, sub] = count

    def waits_for(hop):
        part, phase, k, sub = hop
        if abs(k) > 1:
            return [(part, phase, k - 1 if k > 0 else k + 1, sub)]
        if phase == 0:
            return []
        if phase == 1:
            return [(part, 0, sub[0], ())] if sub[0] else []
        found = []
        for j in offsets_along(SIZES[ORDERS[part][0]]):
            if sub[1]:
                found.append((part, 1, sub[1], (j,)))
            elif j:
                found.append((part, 0, j, ()))
        return found

    needs = {hop: waits_for(hop) for hop in rows}
    done, free, todo = {}, {}, set(rows)
    while todo:
        best = None
        for hop in todo:
            if all(d in done for d in needs[hop]):
                ready = max([done[d] for d in needs[hop]], default=0.0)
                axis = ORDERS[hop[0]][hop[1]]
                start = max(ready, free.get(axis, 0.0))
                key = (start, hop[1], ready, -hop[2], str(hop))
                if best is None or key < best[0]:
                    best = (key, hop, axis, start)
        _, hop, axis, start = best
        free[axis] = start + rows[hop]
        done[hop] = free[axis] + latency
        todo.discard(hop)
    return sorted(rows, key=lambda hop: (done[hop], str(hop))), needs


def coordinates(index):
    return (index // 64, index % 64)


def gather_kernel(
    plan,
    needs,
    shard_ref,
    gain_ref,
    side_ref,
    out_ref,
    gains_ref,
    got_side_ref,
    away,
    came,
    block,
    local_sem,
    gain_local,
    side_local,
    pair_send,
    pair_recv,
    gain_send,
    gain_recv,
    side_send,
    side_recv,
    send_sem,
    recv_sem,
    sib_send,
    sib_recv,
):
    x = lax.axis_index("segment")
    dp = lax.axis_index("dp")
    me = x * 64 + dp
    core = dp % 2
    z = (dp // 2) % SIZES[2]
    y = dp // (2 * SIZES[2])
    here = (x, y, z)
    sign = 1 - 2 * core
    owners = side_ref.shape[0]

    barrier = pltpu.get_barrier_semaphore()

    @pl.loop(1, owners)
    def _(i):
        other = (me + i) % owners
        pl.semaphore_signal(barrier, inc=1, device_id=coordinates(other), device_id_type=MESH)

    rows, width = shard_ref.shape
    half = width // 2
    keep = shard_ref[:, pl.ds(pl.multiple_of(core * half, HD), half)].astype(F32)
    other_half = shard_ref[:, pl.ds(pl.multiple_of((1 - core) * half, HD), half)].astype(F32)
    spare = jnp.zeros((away.shape[0] - rows, half), F32)
    away[...] = jnp.concatenate([other_half, spare], axis=0).astype(BF16)
    gain_copy = pltpu.make_async_copy(gain_ref, gains_ref.at[x], gain_local)
    gain_copy.start()
    side_copy = pltpu.make_async_copy(side_ref.at[me], got_side_ref.at[me], side_local)
    side_copy.start()

    pl.semaphore_wait(barrier, owners - 1)

    def device(at, on):
        return (at[0], (at[1] * SIZES[2] + at[2]) * 2 + on)

    def reach(axis, k, way):
        return (here[axis] + way * k + 2 * SIZES[axis]) % SIZES[axis]

    sibling = device(here, 1 - core)
    pair = pltpu.make_async_remote_copy(
        src_ref=away,
        dst_ref=came,
        send_sem=pair_send,
        recv_sem=pair_recv,
        device_id=sibling,
        device_id_type=MESH,
    )
    pair.start()
    gain_copies = []
    for k in range(1, SIZES[0]):
        copy = pltpu.make_async_remote_copy(
            src_ref=gain_ref,
            dst_ref=gains_ref.at[x],
            send_sem=gain_send.at[k - 1],
            recv_sem=gain_recv.at[k - 1],
            device_id=(reach(0, k, 1), dp),
            device_id_type=MESH,
        )
        copy.start()
        gain_copies.append(copy)
    pair.wait_recv()
    theirs = came[...].astype(F32)[:rows]

    @pl.when(core == 0)
    def _():
        block[...] = jnp.concatenate([keep, theirs], axis=0).astype(BF16)

    @pl.when(core == 1)
    def _():
        block[...] = jnp.concatenate([theirs, keep], axis=0).astype(BF16)

    mine = pltpu.make_async_copy(block, out_ref.at[core, x, y, z], local_sem)
    mine.start()
    mine.wait()

    starts = [sum(PART_ROWS[:part]) for part in range(len(PART_ROWS))]
    number = {hop: i for i, hop in enumerate(plan)}

    def held(hop, travelled, on, way):
        part, phase, _, sub = hop
        order = ORDERS[part]
        at = list(here)
        at[order[phase]] = reach(order[phase], -travelled, way)
        for axis, k in zip(order[:phase], sub):
            at[axis] = slice(None) if k is None else reach(axis, -k, way)
        return out_ref.at[
            on, at[0], at[1], at[2], pl.ds(starts[part], PART_ROWS[part]), :
        ]

    def hop_copy(hop, sending):
        part, phase, k, _ = hop
        axis = ORDERS[part][phase]
        step = 1 if k > 0 else -1
        ref = held(hop, k - step if sending else k, core, sign)
        to = list(here)
        to[axis] = reach(axis, step, sign)
        return pltpu.make_async_remote_copy(
            src_ref=ref,
            dst_ref=ref,
            send_sem=send_sem.at[number[hop]],
            recv_sem=recv_sem.at[number[hop]],
            device_id=device(to, core),
            device_id_type=MESH,
        )

    def share(hop, on, way):
        ref = out_ref.at[on, x, y, z] if hop is None else held(hop, hop[2], on, way)
        index = len(plan) if hop is None else number[hop]
        return pltpu.make_async_remote_copy(
            src_ref=ref,
            dst_ref=ref,
            send_sem=sib_send.at[index],
            recv_sem=sib_recv.at[index],
            device_id=sibling,
            device_id_type=MESH,
        )

    sends = []
    started, arrived = set(), set()

    def launch(copy):
        copy.start()
        sends.append(copy)

    def start_ready():
        for hop in plan:
            if hop not in started and all(d in arrived for d in needs[hop]):
                launch(hop_copy(hop, True))
                started.add(hop)

    start_ready()
    launch(share(None, core, sign))

    @pl.loop(1, owners)
    def _(i):
        other = (me + i) % owners
        pltpu.make_async_remote_copy(
            src_ref=side_ref.at[other],
            dst_ref=got_side_ref.at[me],
            send_sem=side_send,
            recv_sem=side_recv,
            device_id=coordinates(other),
            device_id_type=MESH,
        ).start()

    for hop in plan:
        hop_copy(hop, False).wait_recv()
        arrived.add(hop)
        start_ready()
        launch(share(hop, core, sign))

    for hop in [None] + plan:
        share(hop, 1 - core, -sign).wait_recv()
    for copy in sends:
        copy.wait_send()
    pair.wait_send()
    gain_copy.wait()
    side_copy.wait()
    for k, copy in enumerate(gain_copies):
        copy.wait_send()
        behind = gains_ref.at[reach(0, -(k + 1), 1)]
        pltpu.make_async_copy(behind, behind, gain_recv.at[k]).wait()
    most = got_side_ref.at[pl.ds(0, owners - 1)]
    pltpu.make_async_copy(most, most, side_send).wait()
    pltpu.make_async_copy(most, most, side_recv).wait()


def gather_weights(shard, gain, side):
    rows, width = shard.shape
    plan, needs = gather_plan()
    hops = len(plan)
    half = width // 2
    anywhere = pl.BlockSpec(memory_space=pl.ANY)
    dma = pltpu.SemaphoreType.DMA
    return pl.pallas_call(
        functools.partial(gather_kernel, plan, needs),
        out_shape=(
            jax.ShapeDtypeStruct((2, *SIZES, 2 * rows, half), shard.dtype),
            jax.ShapeDtypeStruct((SIZES[0], *gain.shape), gain.dtype),
            jax.ShapeDtypeStruct(side.shape, side.dtype),
        ),
        in_specs=[pl.BlockSpec(memory_space=pltpu.VMEM), anywhere, anywhere],
        out_specs=(anywhere, anywhere, anywhere),
        scratch_shapes=[
            pltpu.VMEM((64, half), BF16),
            pltpu.VMEM((64, half), BF16),
            pltpu.VMEM((2 * rows, half), BF16),
            dma,
            dma,
            dma,
            dma,
            dma,
            dma((SIZES[0] - 1,)),
            dma((SIZES[0] - 1,)),
            dma,
            dma,
            dma((hops,)),
            dma((hops,)),
            dma((hops + 1,)),
            dma((hops + 1,)),
        ],
        compiler_params=pltpu.CompilerParams(
            collective_id=0, has_side_effects=True, vmem_limit_bytes=16 << 20
        ),
        name="gather_weights",
    )(shard, gain, side)


def teacher_kernel(
    steps,
    items_ref,
    gains_ref,
    weight_ref,
    student_gain_ref,
    out_gain_ref,
    adapter_ref,
    out_ref,
    total,
    act,
    adapter,
    adapter_sem,
):
    step = pl.program_id(0)
    section = step // steps
    inner = step % steps
    depth, half = weight_ref.shape[2] * weight_ref.shape[3], weight_ref.shape[4]
    width = 2 * half
    is_value = section % 2 == 0
    begins = inner == 0
    part = inner % 2
    chunk = inner // 2

    @pl.when(step == 0)
    def _():
        pltpu.make_async_copy(adapter_ref, adapter, adapter_sem).start()
        act[...] = normalize(items_ref[...].astype(F32), gains_ref[0]).astype(BF16)

    @pl.when(begins & (step > 0) & is_value)
    def _():
        hidden = (total[...] * gains_ref[section - 1]).astype(BF16).astype(F32)
        act[...] = normalize(hidden, gains_ref[section]).astype(BF16)

    @pl.when(begins & jnp.logical_not(is_value))
    def _():
        for head in range(width // HD):
            cols = slice(head * HD, (head + 1) * HD)
            values = total[:, cols].astype(BF16).astype(F32)
            scale = lax.rsqrt(jnp.mean(values * values, axis=-1, keepdims=True) + eps)
            act[:, cols] = (values * scale).astype(BF16)

    @pl.when(begins)
    def _():
        total[...] = jnp.zeros_like(total)

    weight = weight_ref[0, 0].reshape(depth, half)

    @pl.when(is_value)
    def _():
        lhs = act[:, pl.ds(pl.multiple_of(chunk * depth, HD), depth)]
        cols = pl.ds(pl.multiple_of(part * half, HD), half)
        total[:, cols] += dot(lhs, weight)

    @pl.when(jnp.logical_not(is_value))
    def _():
        lhs = act[:, pl.ds(pl.multiple_of(part * half, HD), half)]
        cols = pl.ds(pl.multiple_of(chunk * depth, HD), depth)
        total[:, cols] += dot(lhs, weight, ((1,), (1,)))

    @pl.when(step == pl.num_programs(0) - 1)
    def _():
        outcome = (total[...] * gains_ref[section]).astype(BF16).astype(F32)
        act[...] = normalize(outcome, student_gain_ref[...]).astype(BF16)
        pltpu.make_async_copy(adapter_ref, adapter, adapter_sem).wait()
        raw = dot(act[...], adapter[...])
        out_ref[...] = normalize(raw, out_gain_ref[...]).astype(BF16)


def teacher(items, gains, gathered, student_gain, adapter, out_gain):
    rows, width = items.shape
    sections = gathered.shape[1]
    weights = gathered.reshape(2, sections, -1, *gathered.shape[-2:])
    blocks = 8
    steps = 2 * weights.shape[2] // blocks
    whole = lambda *shape: pl.BlockSpec(shape, lambda step: (0,) * len(shape))
    return pl.pallas_call(
        functools.partial(teacher_kernel, steps),
        out_shape=jax.ShapeDtypeStruct((rows, adapter.shape[1]), BF16),
        grid=(sections * steps,),
        in_specs=[
            whole(rows, width),
            whole(sections, 1, width),
            pl.BlockSpec(
                (1, 1, blocks, *weights.shape[-2:]),
                lambda step: (step % 2, step // steps, step % steps // 2, 0, 0),
            ),
            whole(1, width),
            whole(1, adapter.shape[1]),
            pl.BlockSpec(memory_space=pl.ANY),
        ],
        out_specs=whole(rows, adapter.shape[1]),
        scratch_shapes=[
            pltpu.VMEM((rows, width), F32),
            pltpu.VMEM((rows, width), BF16),
            pltpu.VMEM(adapter.shape, BF16),
            pltpu.SemaphoreType.DMA,
        ],
        compiler_params=pltpu.CompilerParams(vmem_limit_bytes=40 << 20),
        name="teacher_chain",
    )(items, gains, weights, student_gain.reshape(1, -1), out_gain.reshape(1, -1), adapter)


def log_softmax(values):
    shifted = values - jnp.max(values, axis=-1, keepdims=True)
    return shifted - jnp.log(jnp.sum(jnp.exp(shifted), axis=-1, keepdims=True))


def pairs_kernel(
    target_ref,
    embed_ref,
    side_ref,
    bank_ref,
    bias_ref,
    neg_ref,
    emb_grad_ref,
    bank_grad_ref,
    kl_ref,
    out_buf,
    got,
    home,
    kl_out,
    kl_home,
    wide,
    slots,
    negatives,
    local_sems,
    send_sem,
    recv_sem,
    back_send,
    back_recv,
    kl_send,
    kl_recv,
):
    me = lax.axis_index("segment") * 64 + lax.axis_index("dp")
    owners, lines, lanes = got.shape
    rows, embed_width = embed_ref.shape
    splits = embed_width // lanes
    picks = target_ref.shape[0]
    capacity = lines // splits
    score_scale = temper * embed_width ** (-0.5)

    barrier = pltpu.get_barrier_semaphore()

    @pl.loop(1, owners)
    def _(i):
        other = (me + i) % owners
        pl.semaphore_signal(barrier, inc=1, device_id=coordinates(other), device_id_type=MESH)

    def send_map(rank):
        slot = lax.broadcasted_iota(jnp.int32, (owners, rows), 0) * capacity + rank
        hit = target_ref[0:1, :] == slot
        for pick in range(1, picks):
            hit = hit | (target_ref[pick : pick + 1, :] == slot)
        return hit.astype(F32).astype(BF16)

    def line(rank, split):
        return pl.ds(rank * splits + split, owners, stride=lines)

    for rank in range(capacity):
        sent = dot(send_map(rank), embed_ref[...])
        for split in range(splits):
            wide[line(rank, split), :] = sent[:, split * lanes : (split + 1) * lanes]
    out_buf[...] = wide[...].reshape(owners, lines, lanes).astype(BF16)

    pl.semaphore_wait(barrier, owners - 1)

    def exchange(src, dst, local, send, recv):
        own = pltpu.make_async_copy(src.at[me], dst.at[me], local)
        own.start()

        @pl.loop(1, owners)
        def _(i):
            other = (me + i) % owners
            pltpu.make_async_remote_copy(
                src_ref=src.at[other],
                dst_ref=dst.at[me],
                send_sem=send,
                recv_sem=recv,
                device_id=coordinates(other),
                device_id_type=MESH,
            ).start()

        return own

    def finish(dst, own, send, recv):
        own.wait()
        most = dst.at[pl.ds(0, owners - 1)]
        pltpu.make_async_copy(most, most, recv).wait()
        pltpu.make_async_copy(most, most, send).wait()

    own = exchange(out_buf, got, local_sems.at[0], send_sem, recv_sem)

    pool = bank_ref.shape[0]
    negs = neg_ref.shape[1]
    chosen = neg_ref[...] == lax.broadcasted_iota(jnp.int32, (pool, negs), 0)
    choose = chosen.astype(F32).astype(BF16)
    negatives[...] = dot(choose, bank_ref[...], ((0,), (0,))).astype(BF16)
    offsets = jnp.sum(jnp.where(chosen, bias_ref[...], 0.0), axis=0, keepdims=True)
    valid = (side_ref[:, 0:1] > 0.5 * UNUSED).astype(F32)
    teacher_log = log_softmax(side_ref[...])
    teacher_prob = jnp.exp(teacher_log)

    finish(got, own, send_sem, recv_sem)
    wide[...] = got[...].astype(F32).reshape(owners * lines, lanes)
    for rank in range(capacity):
        for split in range(splits):
            slots[rank * owners : (rank + 1) * owners, split * lanes : (split + 1) * lanes] = wide[
                line(rank, split), :
            ].astype(BF16)

    logits = dot(slots[...], negatives[...], ((1,), (1,))) * score_scale + offsets
    student_log = log_softmax(logits)
    divergence = jnp.sum(teacher_prob * (teacher_log - student_log), axis=-1, keepdims=True)
    divergence = divergence.astype(BF16).astype(F32)
    lane = lax.broadcasted_iota(jnp.int32, (owners, lanes), 1)
    spread = jnp.zeros((owners, lanes), F32)
    for rank in range(capacity):
        spread = jnp.where(lane == rank, divergence[rank * owners : (rank + 1) * owners], spread)
    kl_out[...] = spread.reshape(owners, 1, lanes)
    kl_own = exchange(kl_out, kl_home, local_sems.at[1], kl_send, kl_recv)

    gap = (valid * (jnp.exp(student_log) - teacher_prob)).astype(BF16)
    for rank in range(capacity):
        grad = dot(gap[rank * owners : (rank + 1) * owners], negatives[...]) * score_scale
        for split in range(splits):
            wide[line(rank, split), :] = grad[:, split * lanes : (split + 1) * lanes]
    out_buf[...] = wide[...].reshape(owners, lines, lanes).astype(BF16)
    own = exchange(out_buf, home, local_sems.at[2], back_send, back_recv)

    rest = dot(gap, slots[...], ((0,), (0,))) * score_scale
    bank_grad = jnp.zeros(bank_grad_ref.shape, F32)
    for _ in range(3):
        term = rest.astype(BF16)
        bank_grad = bank_grad + dot(choose, term)
        rest = rest - term.astype(F32)
    bank_grad_ref[...] = bank_grad

    finish(kl_home, kl_own, kl_send, kl_recv)
    kl_ref[...] = kl_home[...].reshape(owners, lanes)
    finish(home, own, back_send, back_recv)
    wide[...] = home[...].astype(F32).reshape(owners * lines, lanes)
    for rank in range(capacity):
        for split in range(splits):
            slots[rank * owners : (rank + 1) * owners, split * lanes : (split + 1) * lanes] = wide[
                line(rank, split), :
            ].astype(BF16)
    emb_grad = jnp.zeros(emb_grad_ref.shape, F32)
    for rank in range(capacity):
        held = slots[rank * owners : (rank + 1) * owners, :]
        emb_grad = emb_grad + dot(send_map(rank), held, ((0,), (0,)))
    emb_grad_ref[...] = emb_grad


def pairs(target, embedding, side, bank, bank_bias, neg_index, owners, capacity):
    rows, embed_width = embedding.shape
    lines = capacity * embed_width // HD
    vmem = pl.BlockSpec(memory_space=pltpu.VMEM)
    dma = pltpu.SemaphoreType.DMA
    return pl.pallas_call(
        pairs_kernel,
        out_shape=(
            jax.ShapeDtypeStruct((rows, embed_width), F32),
            jax.ShapeDtypeStruct(bank.shape, F32),
            jax.ShapeDtypeStruct((owners, HD), F32),
        ),
        in_specs=[vmem] * 6,
        out_specs=(vmem,) * 3,
        scratch_shapes=[
            pltpu.VMEM((owners, lines, HD), BF16),
            pltpu.VMEM((owners, lines, HD), BF16),
            pltpu.VMEM((owners, lines, HD), BF16),
            pltpu.VMEM((owners, 1, HD), F32),
            pltpu.VMEM((owners, 1, HD), F32),
            pltpu.VMEM((owners * lines, HD), F32),
            pltpu.VMEM((owners * capacity, embed_width), BF16),
            pltpu.VMEM((neg_index.shape[1], embed_width), BF16),
            dma((3,)),
            dma,
            dma,
            dma,
            dma,
            dma,
            dma,
        ],
        compiler_params=pltpu.CompilerParams(
            collective_id=1, has_side_effects=True, vmem_limit_bytes=40 << 20
        ),
        name="pair_exchange",
    )(target, embedding, side, bank, bank_bias.reshape(-1, 1), neg_index)


def shards(
    items,
    section_weights,
    section_gains,
    student_gain,
    adapter,
    out_gain,
    assign,
    teacher_scores,
    bank,
    bank_bias,
    neg_index,
):
    owners = lax.axis_size("segment") * lax.axis_size("dp")
    row_count, pick_count = assign.shape
    pair_count = row_count * pick_count
    capacity = 2
    slot_count = owners * capacity

    pair_cluster = assign.reshape(-1)
    same = pair_cluster[:, None] == pair_cluster[None, :]
    earlier = jnp.arange(pair_count)[:, None] > jnp.arange(pair_count)[None, :]
    pair_rank = jnp.sum((same & earlier).astype(jnp.int32), axis=1)
    target = pair_cluster * capacity + pair_rank
    pick_map = target[None, :] == jnp.arange(slot_count, dtype=jnp.int32)[:, None]
    scores = teacher_scores.reshape(pair_count, -1)
    side = jnp.dot(pick_map.astype(BF16), scores, preferred_element_type=F32)
    side = jnp.where(jnp.any(pick_map, axis=1, keepdims=True), side, UNUSED)
    side = side.reshape(owners, capacity, -1)

    gathered, gains, got_side = gather_weights(
        section_weights[0], section_gains.reshape(1, -1), side
    )
    embedding = teacher(items, gains, gathered, student_gain, adapter, out_gain)
    slot_side = got_side.transpose(1, 0, 2).reshape(slot_count, -1)
    target_rows = target.reshape(row_count, pick_count).T
    emb_grad, bank_grad, owner_kl = pairs(
        target_rows, embedding, slot_side, bank, bank_bias, neg_index, owners, capacity
    )
    slot_kl = owner_kl[:, :capacity].reshape(slot_count)
    row_kl = jnp.sum(jnp.where(pick_map, slot_kl[:, None], 0.0), axis=0)
    row_kl = row_kl.astype(BF16).reshape(row_count, pick_count)
    return (emb_grad, row_kl, bank_grad)


def solution(mesh):
    in_specs = (
        P(("segment", "dp"), None),
        P("segment", "dp", None),
        P("segment", None),
        P(),
        P(),
        P(),
        P(("segment", "dp"), None),
        P(("segment", "dp"), None, None),
        P(("segment", "dp"), None),
        P(("segment", "dp")),
        P(("segment", "dp"), None),
    )
    out_specs = (P(("segment", "dp"), None), P(("segment", "dp"), None), P(("segment", "dp"), None))
    return jax.shard_map(shards, mesh=mesh, in_specs=in_specs, out_specs=out_specs, check_vma=False)
```

```python
import functools

import jax
import jax.numpy as jnp
from jax import lax
from jax.experimental import pallas as pl
from jax.experimental.pallas import tpu as pltpu
from jax.sharding import PartitionSpec as P

HD = 128
MESH = pl.DeviceIdType.MESH
F32 = jnp.float32
BF16 = jnp.bfloat16

eps = 1e-06
temper = 4.0
UNUSED = -1e30

SIZES = (4, 4, 8)
ORDERS = ((0, 1, 2), (2, 1, 0), (0, 2, 1))
PART_ROWS = (32, 48, 32)
GROUPED = (True, False, False)


def dot(a, b, contract=((1,), (0,))):
    return lax.dot_general(a, b, (contract, ((), ())), preferred_element_type=F32)


def normalize(values, scale_row):
    return values * lax.rsqrt(jnp.mean(values * values, axis=-1, keepdims=True) + eps) * scale_row


def offsets_along(size):
    return [0] + list(range(1, size // 2 + 1)) + [-k for k in range(1, size // 2)]


def gather_plan(window=8, latency=140.0, release=60.0):
    rows, needs = {}, {}
    for part, order in enumerate(ORDERS):
        for phase, axis in enumerate(order):
            if phase == 0:
                subs = [()]
            elif phase == 1:
                subs = [(k,) for k in offsets_along(SIZES[order[0]])]
            else:
                firsts = [None] if GROUPED[part] else offsets_along(SIZES[order[0]])
                subs = [(j, k) for j in firsts for k in offsets_along(SIZES[order[1]])]
            for sub in subs:
                count = PART_ROWS[part] * (SIZES[order[0]] if None in sub else 1)
                for k in offsets_along(SIZES[axis]):
                    if k:
                        rows[part, phase, k, sub] = count

    def waits_for(hop):
        part, phase, k, sub = hop
        if abs(k) > 1:
            return [(part, phase, k - 1 if k > 0 else k + 1, sub)]
        if phase == 0:
            return []
        if phase == 1:
            return [(part, 0, sub[0], ())] if sub[0] else []
        found = []
        for j in offsets_along(SIZES[ORDERS[part][0]]) if sub[0] is None else [sub[0]]:
            if sub[1]:
                found.append((part, 1, sub[1], (j,)))
            elif j:
                found.append((part, 0, j, ()))
        return found

    for hop in rows:
        needs[hop] = waits_for(hop)

    def axis_of(hop):
        return ORDERS[hop[0]][hop[1]]

    def lane_of(hop):
        return (axis_of(hop), hop[2] > 0)

    def urgency(hop):
        size = SIZES[axis_of(hop)]
        rest = size // 2 - hop[2] if hop[2] > 0 else size // 2 - 1 + hop[2]
        return (hop[1], -rest, str(hop))

    queues = {(axis, long_way): [] for axis in range(3) for long_way in (True, False)}
    flying = dict.fromkeys(queues, 0)
    for hop in rows:
        if not needs[hop]:
            queues[lane_of(hop)].append(hop)
    events, active, landing, leaving, came = [], {}, {}, {}, set()
    now = 0.0
    while True:
        for lane, queue in queues.items():
            while queue and flying[lane] < window:
                queue.sort(key=urgency)
                hop = queue.pop(0)
                active[hop] = float(rows[hop])
                flying[lane] += 1
                events.append((round(now, 3), 2, str(hop), "start", hop))
        if not (active or landing or leaving):
            break
        load = [0, 0, 0]
        for hop in active:
            load[axis_of(hop)] += 1
        step = min(
            [left * load[axis_of(hop)] for hop, left in active.items()]
            + [end - now for end in landing.values()]
            + [end - now for end in leaving.values()]
        )
        now += step
        for hop in list(active):
            active[hop] -= step / load[axis_of(hop)]
            if active[hop] < 1e-6:
                del active[hop]
                landing[hop] = now + latency
                leaving[hop] = now + release
        for hop in [h for h, end in leaving.items() if end <= now + 1e-6]:
            del leaving[hop]
            flying[lane_of(hop)] -= 1
            events.append((round(now, 3), 1, str(hop), "sent", hop))
        for hop in [h for h, end in landing.items() if end <= now + 1e-6]:
            del landing[hop]
            came.add(hop)
            events.append((round(now, 3), 0, str(hop), "came", hop))
            for user in rows:
                if hop in needs[user] and all(d in came for d in needs[user]):
                    queues[lane_of(user)].append(user)
    begun = {(lane_of(hop), at) for at, _, _, kind, hop in events if kind == "start"}
    return [
        (kind, hop)
        for at, _, _, kind, hop in sorted(events, key=lambda event: event[:3])
        if kind != "sent" or (lane_of(hop), at) in begun
    ]


def coordinates(index):
    return (index // 64, index % 64)


def gather_kernel(
    events,
    shard_ref,
    gain_ref,
    side_ref,
    out_ref,
    gains_ref,
    got_side_ref,
    away,
    came,
    block,
    local_sem,
    gain_local,
    side_local,
    pair_send,
    pair_recv,
    gain_send,
    gain_recv,
    side_send,
    side_recv,
    send_sem,
    recv_sem,
    sib_send,
    sib_recv,
):
    x = lax.axis_index("segment")
    dp = lax.axis_index("dp")
    me = x * 64 + dp
    core = dp % 2
    z = (dp // 2) % SIZES[2]
    y = dp // (2 * SIZES[2])
    here = (x, y, z)
    sign = 1 - 2 * core
    owners = side_ref.shape[0]

    barrier = pltpu.get_barrier_semaphore()

    @pl.loop(1, owners)
    def _(i):
        other = (me + i) % owners
        pl.semaphore_signal(barrier, inc=1, device_id=coordinates(other), device_id_type=MESH)

    rows, width = shard_ref.shape
    half = width // 2
    keep = shard_ref[:, pl.ds(pl.multiple_of(core * half, HD), half)].astype(F32)
    other_half = shard_ref[:, pl.ds(pl.multiple_of((1 - core) * half, HD), half)].astype(F32)
    spare = jnp.zeros((away.shape[0] - rows, half), F32)
    away[...] = jnp.concatenate([other_half, spare], axis=0).astype(BF16)
    gain_copy = pltpu.make_async_copy(gain_ref, gains_ref.at[x], gain_local)
    gain_copy.start()
    side_copy = pltpu.make_async_copy(side_ref.at[me], got_side_ref.at[me], side_local)
    side_copy.start()

    pl.semaphore_wait(barrier, owners - 1)

    def device(at, on):
        return (at[0], (at[1] * SIZES[2] + at[2]) * 2 + on)

    def reach(axis, k, way):
        return (here[axis] + way * k + 2 * SIZES[axis]) % SIZES[axis]

    sibling = device(here, 1 - core)
    pair = pltpu.make_async_remote_copy(
        src_ref=away,
        dst_ref=came,
        send_sem=pair_send,
        recv_sem=pair_recv,
        device_id=sibling,
        device_id_type=MESH,
    )
    pair.start()
    gain_copies = []
    for k in range(1, SIZES[0]):
        copy = pltpu.make_async_remote_copy(
            src_ref=gain_ref,
            dst_ref=gains_ref.at[x],
            send_sem=gain_send.at[k - 1],
            recv_sem=gain_recv.at[k - 1],
            device_id=(reach(0, k, 1), dp),
            device_id_type=MESH,
        )
        copy.start()
        gain_copies.append(copy)
    pair.wait_recv()
    theirs = came[...].astype(F32)[:rows]

    @pl.when(core == 0)
    def _():
        block[...] = jnp.concatenate([keep, theirs], axis=0).astype(BF16)

    @pl.when(core == 1)
    def _():
        block[...] = jnp.concatenate([theirs, keep], axis=0).astype(BF16)

    mine = pltpu.make_async_copy(block, out_ref.at[core, x, y, z], local_sem)
    mine.start()
    mine.wait()

    starts = [sum(PART_ROWS[:part]) for part in range(len(PART_ROWS))]
    plan = [hop for kind, hop in events if kind == "came"]
    number = {hop: i for i, hop in enumerate(plan)}

    def held(hop, travelled, on, way):
        part, phase, _, sub = hop
        order = ORDERS[part]
        at = list(here)
        at[order[phase]] = reach(order[phase], -travelled, way)
        for axis, k in zip(order[:phase], sub):
            at[axis] = slice(None) if k is None else reach(axis, -k, way)
        return out_ref.at[
            on, at[0], at[1], at[2], pl.ds(starts[part], PART_ROWS[part]), :
        ]

    def hop_copy(hop, sending):
        part, phase, k, _ = hop
        axis = ORDERS[part][phase]
        step = 1 if k > 0 else -1
        ref = held(hop, k - step if sending else k, core, sign)
        to = list(here)
        to[axis] = reach(axis, step, sign)
        return pltpu.make_async_remote_copy(
            src_ref=ref,
            dst_ref=ref,
            send_sem=send_sem.at[number[hop]],
            recv_sem=recv_sem.at[number[hop]],
            device_id=device(to, core),
            device_id_type=MESH,
        )

    def share(hop, on, way):
        ref = out_ref.at[on, x, y, z] if hop is None else held(hop, hop[2], on, way)
        index = len(plan) if hop is None else number[hop]
        return pltpu.make_async_remote_copy(
            src_ref=ref,
            dst_ref=ref,
            send_sem=sib_send.at[index],
            recv_sem=sib_recv.at[index],
            device_id=sibling,
            device_id_type=MESH,
        )

    def send_side(begin, end):
        @pl.loop(begin, end)
        def _(i):
            other = (me + i) % owners
            pltpu.make_async_remote_copy(
                src_ref=side_ref.at[other],
                dst_ref=got_side_ref.at[me],
                send_sem=side_send,
                recv_sem=side_recv,
                device_id=coordinates(other),
                device_id_type=MESH,
            ).start()

    shares = [share(None, core, sign)]
    shares[0].start()
    copies = {}
    pieces = [(begin, min(begin + 32, owners)) for begin in range(1, owners, 32)]
    for kind, hop in events:
        if kind == "start":
            copies[hop] = hop_copy(hop, True)
            copies[hop].start()
        elif kind == "sent":
            copies.pop(hop).wait_send()
        else:
            hop_copy(hop, False).wait_recv()
            if len(shares) > 60 and len(shares) % 16 == 0 and pieces:
                send_side(*pieces.pop(0))
            shares.append(share(hop, core, sign))
            shares[-1].start()

    for hop in [None] + plan:
        share(hop, 1 - core, -sign).wait_recv()
    for copy in shares + list(copies.values()):
        copy.wait_send()
    pair.wait_send()
    gain_copy.wait()
    side_copy.wait()
    for k, copy in enumerate(gain_copies):
        copy.wait_send()
        behind = gains_ref.at[reach(0, -(k + 1), 1)]
        pltpu.make_async_copy(behind, behind, gain_recv.at[k]).wait()
    most = got_side_ref.at[pl.ds(0, owners - 1)]
    pltpu.make_async_copy(most, most, side_send).wait()
    pltpu.make_async_copy(most, most, side_recv).wait()


def gather_weights(shard, gain, side):
    rows, width = shard.shape
    events = gather_plan()
    hops = sum(kind == "came" for kind, _ in events)
    half = width // 2
    anywhere = pl.BlockSpec(memory_space=pl.ANY)
    dma = pltpu.SemaphoreType.DMA
    return pl.pallas_call(
        functools.partial(gather_kernel, events),
        out_shape=(
            jax.ShapeDtypeStruct((2, *SIZES, 2 * rows, half), shard.dtype),
            jax.ShapeDtypeStruct((SIZES[0], *gain.shape), gain.dtype),
            jax.ShapeDtypeStruct(side.shape, side.dtype),
        ),
        in_specs=[pl.BlockSpec(memory_space=pltpu.VMEM), anywhere, anywhere],
        out_specs=(anywhere, anywhere, anywhere),
        scratch_shapes=[
            pltpu.VMEM((64, half), BF16),
            pltpu.VMEM((64, half), BF16),
            pltpu.VMEM((2 * rows, half), BF16),
            dma,
            dma,
            dma,
            dma,
            dma,
            dma((SIZES[0] - 1,)),
            dma((SIZES[0] - 1,)),
            dma,
            dma,
            dma((hops,)),
            dma((hops,)),
            dma((hops + 1,)),
            dma((hops + 1,)),
        ],
        compiler_params=pltpu.CompilerParams(
            collective_id=0, has_side_effects=True, vmem_limit_bytes=16 << 20
        ),
        name="gather_weights",
    )(shard, gain, side)


def teacher_kernel(
    steps,
    items_ref,
    gains_ref,
    left_ref,
    right_ref,
    student_gain_ref,
    out_gain_ref,
    adapter_ref,
    out_ref,
    total,
    act,
    adapter,
    adapter_sem,
):
    step = pl.program_id(0)
    section = step // steps
    chunk = step % steps
    depth, half = left_ref.shape[2] * left_ref.shape[3], left_ref.shape[4]
    width = 2 * half
    is_value = section % 2 == 0
    is_output = section % 2 == 1
    begins = chunk == 0

    @pl.when(step == 0)
    def _():
        pltpu.make_async_copy(adapter_ref, adapter, adapter_sem).start()
        act[...] = normalize(items_ref[...].astype(F32), gains_ref[0]).astype(BF16)

    @pl.when(begins & (step > 0) & is_value)
    def _():
        hidden = (total[...] * gains_ref[section - 1]).astype(BF16).astype(F32)
        act[...] = normalize(hidden, gains_ref[section]).astype(BF16)

    @pl.when(begins & is_output)
    def _():
        for head in range(width // HD):
            cols = slice(head * HD, (head + 1) * HD)
            values = total[:, cols].astype(BF16).astype(F32)
            scale = lax.rsqrt(jnp.mean(values * values, axis=-1, keepdims=True) + eps)
            act[:, cols] = (values * scale).astype(BF16)

    left = left_ref[0, 0].reshape(depth, half)
    right = right_ref[0, 0].reshape(depth, half)
    place = pl.ds(pl.multiple_of(chunk * depth, HD), depth)

    @pl.when(begins & is_value)
    def _():
        total[:, :half] = dot(act[:, :depth], left)
        total[:, half:width] = dot(act[:, :depth], right)

    @pl.when((chunk > 0) & is_value)
    def _():
        total[:, :half] += dot(act[:, place], left)
        total[:, half:width] += dot(act[:, place], right)

    @pl.when(is_output)
    def _():
        total[:, place] = dot(act[:, :half], left, ((1,), (1,))) + dot(
            act[:, half:width], right, ((1,), (1,))
        )

    @pl.when(step == pl.num_programs(0) - 1)
    def _():
        outcome = (total[...] * gains_ref[section]).astype(BF16).astype(F32)
        act[...] = normalize(outcome, student_gain_ref[...]).astype(BF16)
        pltpu.make_async_copy(adapter_ref, adapter, adapter_sem).wait()
        raw = dot(act[...], adapter[...])
        out_ref[...] = normalize(raw, out_gain_ref[...]).astype(BF16)


def teacher(items, gains, gathered, student_gain, adapter, out_gain):
    rows, width = items.shape
    sections = gathered.shape[1]
    weights = gathered.reshape(2, sections, -1, *gathered.shape[-2:])
    blocks = 16
    steps = weights.shape[2] // blocks
    whole = lambda *shape: pl.BlockSpec(shape, lambda step: (0,) * len(shape))

    def half(part):
        return pl.BlockSpec(
            (1, 1, blocks, *weights.shape[-2:]),
            lambda step: (part, step // steps, step % steps, 0, 0),
        )

    return pl.pallas_call(
        functools.partial(teacher_kernel, steps),
        out_shape=jax.ShapeDtypeStruct((rows, adapter.shape[1]), BF16),
        grid=(sections * steps,),
        in_specs=[
            whole(rows, width),
            whole(sections, 1, width),
            half(0),
            half(1),
            whole(1, width),
            whole(1, adapter.shape[1]),
            pl.BlockSpec(memory_space=pl.ANY),
        ],
        out_specs=whole(rows, adapter.shape[1]),
        scratch_shapes=[
            pltpu.VMEM((rows, width), F32),
            pltpu.VMEM((rows, width), BF16),
            pltpu.VMEM(adapter.shape, BF16),
            pltpu.SemaphoreType.DMA,
        ],
        compiler_params=pltpu.CompilerParams(vmem_limit_bytes=59 << 20),
        name="teacher_chain",
    )(items, gains, weights, weights, student_gain.reshape(1, -1), out_gain.reshape(1, -1), adapter)


def log_softmax(values):
    shifted = values - jnp.max(values, axis=-1, keepdims=True)
    return shifted - jnp.log(jnp.sum(jnp.exp(shifted), axis=-1, keepdims=True))


def pairs_kernel(
    target_ref,
    embed_ref,
    side_ref,
    bank_ref,
    bias_ref,
    neg_ref,
    emb_grad_ref,
    bank_grad_ref,
    kl_ref,
    out_buf,
    got,
    home,
    kl_out,
    kl_home,
    wide,
    slots,
    negatives,
    local_sems,
    send_sem,
    recv_sem,
    back_send,
    back_recv,
    kl_send,
    kl_recv,
):
    me = lax.axis_index("segment") * 64 + lax.axis_index("dp")
    owners, lines, lanes = got.shape
    rows, embed_width = embed_ref.shape
    splits = embed_width // lanes
    picks = target_ref.shape[0]
    capacity = lines // splits
    score_scale = temper * embed_width ** (-0.5)

    barrier = pltpu.get_barrier_semaphore()

    @pl.loop(1, owners)
    def _(i):
        other = (me + i) % owners
        pl.semaphore_signal(barrier, inc=1, device_id=coordinates(other), device_id_type=MESH)

    def send_map(rank):
        slot = lax.broadcasted_iota(jnp.int32, (owners, rows), 0) * capacity + rank
        hit = target_ref[0:1, :] == slot
        for pick in range(1, picks):
            hit = hit | (target_ref[pick : pick + 1, :] == slot)
        return hit.astype(F32).astype(BF16)

    def line(rank, split):
        return pl.ds(rank * splits + split, owners, stride=lines)

    for rank in range(capacity):
        sent = dot(send_map(rank), embed_ref[...])
        for split in range(splits):
            wide[line(rank, split), :] = sent[:, split * lanes : (split + 1) * lanes]
    out_buf[...] = wide[...].reshape(owners, lines, lanes).astype(BF16)

    pl.semaphore_wait(barrier, owners - 1)

    def exchange(src, dst, local, send, recv):
        own = pltpu.make_async_copy(src.at[me], dst.at[me], local)
        own.start()

        @pl.loop(1, owners)
        def _(i):
            other = (me + i) % owners
            pltpu.make_async_remote_copy(
                src_ref=src.at[other],
                dst_ref=dst.at[me],
                send_sem=send,
                recv_sem=recv,
                device_id=coordinates(other),
                device_id_type=MESH,
            ).start()

        return own

    def finish(dst, own, send, recv):
        own.wait()
        most = dst.at[pl.ds(0, owners - 1)]
        pltpu.make_async_copy(most, most, recv).wait()
        pltpu.make_async_copy(most, most, send).wait()

    own = exchange(out_buf, got, local_sems.at[0], send_sem, recv_sem)

    pool = bank_ref.shape[0]
    negs = neg_ref.shape[1]
    chosen = neg_ref[...] == lax.broadcasted_iota(jnp.int32, (pool, negs), 0)
    choose = chosen.astype(F32).astype(BF16)
    negatives[...] = dot(choose, bank_ref[...], ((0,), (0,))).astype(BF16)
    offsets = jnp.sum(jnp.where(chosen, bias_ref[...], 0.0), axis=0, keepdims=True)
    valid = (side_ref[:, 0:1] > 0.5 * UNUSED).astype(F32)
    teacher_log = log_softmax(side_ref[...])
    teacher_prob = jnp.exp(teacher_log)

    finish(got, own, send_sem, recv_sem)
    wide[...] = got[...].astype(F32).reshape(owners * lines, lanes)
    for rank in range(capacity):
        for split in range(splits):
            slots[rank * owners : (rank + 1) * owners, split * lanes : (split + 1) * lanes] = wide[
                line(rank, split), :
            ].astype(BF16)

    logits = dot(slots[...], negatives[...], ((1,), (1,))) * score_scale + offsets
    student_log = log_softmax(logits)
    divergence = jnp.sum(teacher_prob * (teacher_log - student_log), axis=-1, keepdims=True)
    divergence = divergence.astype(BF16).astype(F32)
    lane = lax.broadcasted_iota(jnp.int32, (owners, lanes), 1)
    spread = jnp.zeros((owners, lanes), F32)
    for rank in range(capacity):
        spread = jnp.where(lane == rank, divergence[rank * owners : (rank + 1) * owners], spread)
    kl_out[...] = spread.reshape(owners, 1, lanes)
    kl_own = exchange(kl_out, kl_home, local_sems.at[1], kl_send, kl_recv)

    gap = (valid * (jnp.exp(student_log) - teacher_prob)).astype(BF16)
    for rank in range(capacity):
        grad = dot(gap[rank * owners : (rank + 1) * owners], negatives[...]) * score_scale
        for split in range(splits):
            wide[line(rank, split), :] = grad[:, split * lanes : (split + 1) * lanes]
    out_buf[...] = wide[...].reshape(owners, lines, lanes).astype(BF16)
    own = exchange(out_buf, home, local_sems.at[2], back_send, back_recv)

    rest = dot(gap, slots[...], ((0,), (0,))) * score_scale
    bank_grad = jnp.zeros(bank_grad_ref.shape, F32)
    for _ in range(3):
        term = rest.astype(BF16)
        bank_grad = bank_grad + dot(choose, term)
        rest = rest - term.astype(F32)
    bank_grad_ref[...] = bank_grad

    finish(kl_home, kl_own, kl_send, kl_recv)
    kl_ref[...] = kl_home[...].reshape(owners, lanes)
    finish(home, own, back_send, back_recv)
    wide[...] = home[...].astype(F32).reshape(owners * lines, lanes)
    for rank in range(capacity):
        for split in range(splits):
            slots[rank * owners : (rank + 1) * owners, split * lanes : (split + 1) * lanes] = wide[
                line(rank, split), :
            ].astype(BF16)
    emb_grad = jnp.zeros(emb_grad_ref.shape, F32)
    for rank in range(capacity):
        held = slots[rank * owners : (rank + 1) * owners, :]
        emb_grad = emb_grad + dot(send_map(rank), held, ((0,), (0,)))
    emb_grad_ref[...] = emb_grad


def pairs(target, embedding, side, bank, bank_bias, neg_index, owners, capacity):
    rows, embed_width = embedding.shape
    lines = capacity * embed_width // HD
    vmem = pl.BlockSpec(memory_space=pltpu.VMEM)
    dma = pltpu.SemaphoreType.DMA
    return pl.pallas_call(
        pairs_kernel,
        out_shape=(
            jax.ShapeDtypeStruct((rows, embed_width), F32),
            jax.ShapeDtypeStruct(bank.shape, F32),
            jax.ShapeDtypeStruct((owners, HD), F32),
        ),
        in_specs=[vmem] * 6,
        out_specs=(vmem,) * 3,
        scratch_shapes=[
            pltpu.VMEM((owners, lines, HD), BF16),
            pltpu.VMEM((owners, lines, HD), BF16),
            pltpu.VMEM((owners, lines, HD), BF16),
            pltpu.VMEM((owners, 1, HD), F32),
            pltpu.VMEM((owners, 1, HD), F32),
            pltpu.VMEM((owners * lines, HD), F32),
            pltpu.VMEM((owners * capacity, embed_width), BF16),
            pltpu.VMEM((neg_index.shape[1], embed_width), BF16),
            dma((3,)),
            dma,
            dma,
            dma,
            dma,
            dma,
            dma,
        ],
        compiler_params=pltpu.CompilerParams(
            collective_id=1, has_side_effects=True, vmem_limit_bytes=40 << 20
        ),
        name="pair_exchange",
    )(target, embedding, side, bank, bank_bias.reshape(-1, 1), neg_index)


def shards(
    items,
    section_weights,
    section_gains,
    student_gain,
    adapter,
    out_gain,
    assign,
    teacher_scores,
    bank,
    bank_bias,
    neg_index,
):
    owners = lax.axis_size("segment") * lax.axis_size("dp")
    row_count, pick_count = assign.shape
    pair_count = row_count * pick_count
    capacity = 2
    slot_count = owners * capacity

    pair_cluster = assign.reshape(-1)
    same = pair_cluster[:, None] == pair_cluster[None, :]
    earlier = jnp.arange(pair_count)[:, None] > jnp.arange(pair_count)[None, :]
    pair_rank = jnp.sum((same & earlier).astype(jnp.int32), axis=1)
    target = pair_cluster * capacity + pair_rank
    pick_map = target[None, :] == jnp.arange(slot_count, dtype=jnp.int32)[:, None]
    scores = teacher_scores.reshape(pair_count, -1)
    side = jnp.dot(pick_map.astype(BF16), scores, preferred_element_type=F32)
    side = jnp.where(jnp.any(pick_map, axis=1, keepdims=True), side, UNUSED)
    side = side.reshape(owners, capacity, -1)

    gathered, gains, got_side = gather_weights(
        section_weights[0], section_gains.reshape(1, -1), side
    )
    embedding = teacher(items, gains, gathered, student_gain, adapter, out_gain)
    slot_side = got_side.transpose(1, 0, 2).reshape(slot_count, -1)
    target_rows = target.reshape(row_count, pick_count).T
    emb_grad, bank_grad, owner_kl = pairs(
        target_rows, embedding, slot_side, bank, bank_bias, neg_index, owners, capacity
    )
    slot_kl = owner_kl[:, :capacity].reshape(slot_count)
    row_kl = jnp.sum(jnp.where(pick_map, slot_kl[:, None], 0.0), axis=0)
    row_kl = row_kl.astype(BF16).reshape(row_count, pick_count)
    return (emb_grad, row_kl, bank_grad)


def solution(mesh):
    in_specs = (
        P(("segment", "dp"), None),
        P("segment", "dp", None),
        P("segment", None),
        P(),
        P(),
        P(),
        P(("segment", "dp"), None),
        P(("segment", "dp"), None, None),
        P(("segment", "dp"), None),
        P(("segment", "dp")),
        P(("segment", "dp"), None),
    )
    out_specs = (P(("segment", "dp"), None), P(("segment", "dp"), None), P(("segment", "dp"), None))
    return jax.shard_map(shards, mesh=mesh, in_specs=in_specs, out_specs=out_specs, check_vma=False)
```

```python
import functools

import jax
import jax.numpy as jnp
from jax import lax
from jax.experimental import pallas as pl
from jax.experimental.pallas import tpu as pltpu
from jax.sharding import PartitionSpec as P

HD = 128
MESH = pl.DeviceIdType.MESH
F32 = jnp.float32
BF16 = jnp.bfloat16

eps = 1e-06
temper = 4.0
UNUSED = -1e30

SIZES = (4, 4, 8)
ORDERS = ((0, 1, 2), (2, 1, 0), (0, 2, 1))
PART_ROWS = (32, 48, 32)
GROUPED = (True, False, False)


def dot(a, b, contract=((1,), (0,))):
    return lax.dot_general(a, b, (contract, ((), ())), preferred_element_type=F32)


def normalize(values, scale_row):
    return values * lax.rsqrt(jnp.mean(values * values, axis=-1, keepdims=True) + eps) * scale_row


def offsets_along(size):
    return [0] + list(range(1, size // 2 + 1)) + [-k for k in range(1, size // 2)]


def gather_plan(window=8, latency=140.0, release=60.0):
    rows, needs = {}, {}
    for part, order in enumerate(ORDERS):
        for phase, axis in enumerate(order):
            if phase == 0:
                subs = [()]
            elif phase == 1:
                subs = [(k,) for k in offsets_along(SIZES[order[0]])]
            else:
                firsts = [None] if GROUPED[part] else offsets_along(SIZES[order[0]])
                subs = [(j, k) for j in firsts for k in offsets_along(SIZES[order[1]])]
            for sub in subs:
                count = PART_ROWS[part] * (SIZES[order[0]] if None in sub else 1)
                for k in offsets_along(SIZES[axis]):
                    if k:
                        rows[part, phase, k, sub] = count

    def waits_for(hop):
        part, phase, k, sub = hop
        if abs(k) > 1:
            return [(part, phase, k - 1 if k > 0 else k + 1, sub)]
        if phase == 0:
            return []
        if phase == 1:
            return [(part, 0, sub[0], ())] if sub[0] else []
        found = []
        for j in offsets_along(SIZES[ORDERS[part][0]]) if sub[0] is None else [sub[0]]:
            if sub[1]:
                found.append((part, 1, sub[1], (j,)))
            elif j:
                found.append((part, 0, j, ()))
        return found

    for hop in rows:
        needs[hop] = waits_for(hop)

    def axis_of(hop):
        return ORDERS[hop[0]][hop[1]]

    def lane_of(hop):
        return (axis_of(hop), hop[2] > 0)

    def urgency(hop):
        size = SIZES[axis_of(hop)]
        rest = size // 2 - hop[2] if hop[2] > 0 else size // 2 - 1 + hop[2]
        return (hop[1], -rest, str(hop))

    queues = {(axis, long_way): [] for axis in range(3) for long_way in (True, False)}
    flying = dict.fromkeys(queues, 0)
    for hop in rows:
        if not needs[hop]:
            queues[lane_of(hop)].append(hop)
    events, active, landing, leaving, came = [], {}, {}, {}, set()
    now = 0.0
    while True:
        for lane, queue in queues.items():
            while queue and flying[lane] < window:
                queue.sort(key=urgency)
                hop = queue.pop(0)
                active[hop] = float(rows[hop])
                flying[lane] += 1
                events.append((round(now, 3), 2, str(hop), "start", hop))
        if not (active or landing or leaving):
            break
        load = [0, 0, 0]
        for hop in active:
            load[axis_of(hop)] += 1
        step = min(
            [left * load[axis_of(hop)] for hop, left in active.items()]
            + [end - now for end in landing.values()]
            + [end - now for end in leaving.values()]
        )
        now += step
        for hop in list(active):
            active[hop] -= step / load[axis_of(hop)]
            if active[hop] < 1e-6:
                del active[hop]
                landing[hop] = now + latency
                leaving[hop] = now + release
        for hop in [h for h, end in leaving.items() if end <= now + 1e-6]:
            del leaving[hop]
            flying[lane_of(hop)] -= 1
            events.append((round(now, 3), 1, str(hop), "sent", hop))
        for hop in [h for h, end in landing.items() if end <= now + 1e-6]:
            del landing[hop]
            came.add(hop)
            events.append((round(now, 3), 0, str(hop), "came", hop))
            for user in rows:
                if hop in needs[user] and all(d in came for d in needs[user]):
                    queues[lane_of(user)].append(user)
    begun = {(lane_of(hop), at) for at, _, _, kind, hop in events if kind == "start"}
    return [
        (kind, hop)
        for at, _, _, kind, hop in sorted(events, key=lambda event: event[:3])
        if kind != "sent" or (lane_of(hop), at) in begun
    ]


def coordinates(index):
    return (index // 64, index % 64)


def gather_kernel(
    events,
    shard_ref,
    gain_ref,
    side_ref,
    out_ref,
    gains_ref,
    got_side_ref,
    away,
    came,
    block,
    local_sem,
    gain_local,
    side_local,
    pair_send,
    pair_recv,
    gain_send,
    gain_recv,
    side_send,
    side_recv,
    send_sem,
    recv_sem,
    sib_send,
    sib_recv,
):
    x = lax.axis_index("segment")
    dp = lax.axis_index("dp")
    me = x * 64 + dp
    core = dp % 2
    z = (dp // 2) % SIZES[2]
    y = dp // (2 * SIZES[2])
    here = (x, y, z)
    sign = 1 - 2 * core
    owners = side_ref.shape[0]

    barrier = pltpu.get_barrier_semaphore()

    @pl.loop(1, owners)
    def _(i):
        other = (me + i) % owners
        pl.semaphore_signal(barrier, inc=1, device_id=coordinates(other), device_id_type=MESH)

    rows, width = shard_ref.shape
    half = width // 2
    keep = shard_ref[:, pl.ds(pl.multiple_of(core * half, HD), half)].astype(F32)
    other_half = shard_ref[:, pl.ds(pl.multiple_of((1 - core) * half, HD), half)].astype(F32)
    spare = jnp.zeros((away.shape[0] - rows, half), F32)
    away[...] = jnp.concatenate([other_half, spare], axis=0).astype(BF16)
    gain_copy = pltpu.make_async_copy(gain_ref, gains_ref.at[x], gain_local)
    gain_copy.start()
    side_copy = pltpu.make_async_copy(side_ref.at[me], got_side_ref.at[me], side_local)
    side_copy.start()

    pl.semaphore_wait(barrier, owners - 1)

    def device(at, on):
        return (at[0], (at[1] * SIZES[2] + at[2]) * 2 + on)

    def reach(axis, k, way):
        return (here[axis] + way * k + 2 * SIZES[axis]) % SIZES[axis]

    sibling = device(here, 1 - core)
    pair = pltpu.make_async_remote_copy(
        src_ref=away,
        dst_ref=came,
        send_sem=pair_send,
        recv_sem=pair_recv,
        device_id=sibling,
        device_id_type=MESH,
    )
    pair.start()
    gain_copies = []
    for k in range(1, SIZES[0]):
        copy = pltpu.make_async_remote_copy(
            src_ref=gain_ref,
            dst_ref=gains_ref.at[x],
            send_sem=gain_send.at[k - 1],
            recv_sem=gain_recv.at[k - 1],
            device_id=(reach(0, k, 1), dp),
            device_id_type=MESH,
        )
        copy.start()
        gain_copies.append(copy)
    pair.wait_recv()
    theirs = came[...].astype(F32)[:rows]

    @pl.when(core == 0)
    def _():
        block[...] = jnp.concatenate([keep, theirs], axis=0).astype(BF16)

    @pl.when(core == 1)
    def _():
        block[...] = jnp.concatenate([theirs, keep], axis=0).astype(BF16)

    mine = pltpu.make_async_copy(block, out_ref.at[core, x, y, z], local_sem)
    mine.start()
    mine.wait()

    starts = [sum(PART_ROWS[:part]) for part in range(len(PART_ROWS))]
    plan = [hop for kind, hop in events if kind == "came"]
    number = {hop: i for i, hop in enumerate(plan)}

    def held(hop, travelled, on, way):
        part, phase, _, sub = hop
        order = ORDERS[part]
        at = list(here)
        at[order[phase]] = reach(order[phase], -travelled, way)
        for axis, k in zip(order[:phase], sub):
            at[axis] = slice(None) if k is None else reach(axis, -k, way)
        return out_ref.at[
            on, at[0], at[1], at[2], pl.ds(starts[part], PART_ROWS[part]), :
        ]

    def hop_copy(hop, sending):
        part, phase, k, _ = hop
        axis = ORDERS[part][phase]
        step = 1 if k > 0 else -1
        ref = held(hop, k - step if sending else k, core, sign)
        to = list(here)
        to[axis] = reach(axis, step, sign)
        return pltpu.make_async_remote_copy(
            src_ref=ref,
            dst_ref=ref,
            send_sem=send_sem.at[number[hop]],
            recv_sem=recv_sem.at[number[hop]],
            device_id=device(to, core),
            device_id_type=MESH,
        )

    def share(hop, on, way):
        ref = out_ref.at[on, x, y, z] if hop is None else held(hop, hop[2], on, way)
        index = len(plan) if hop is None else number[hop]
        return pltpu.make_async_remote_copy(
            src_ref=ref,
            dst_ref=ref,
            send_sem=sib_send.at[index],
            recv_sem=sib_recv.at[index],
            device_id=sibling,
            device_id_type=MESH,
        )

    def send_side(begin, end):
        @pl.loop(begin, end)
        def _(i):
            other = (me + i) % owners
            pltpu.make_async_remote_copy(
                src_ref=side_ref.at[other],
                dst_ref=got_side_ref.at[me],
                send_sem=side_send,
                recv_sem=side_recv,
                device_id=coordinates(other),
                device_id_type=MESH,
            ).start()

    shares = [share(None, core, sign)]
    shares[0].start()
    copies = {}
    pieces = [(begin, min(begin + 32, owners)) for begin in range(1, owners, 32)]
    newest = []

    def pass_on():
        for hop in newest:
            shares.append(share(hop, core, sign))
            shares[-1].start()
            if len(shares) > 60 and len(shares) % 16 == 0 and pieces:
                send_side(*pieces.pop(0))
        newest.clear()

    for kind, hop in events:
        if kind == "start":
            copies[hop] = hop_copy(hop, True)
            copies[hop].start()
        elif kind == "sent":
            copies.pop(hop).wait_send()
        else:
            pass_on()
            hop_copy(hop, False).wait_recv()
            newest.append(hop)

    pass_on()
    for hop in [None] + plan:
        share(hop, 1 - core, -sign).wait_recv()
    for copy in shares + list(copies.values()):
        copy.wait_send()
    pair.wait_send()
    gain_copy.wait()
    side_copy.wait()
    for k, copy in enumerate(gain_copies):
        copy.wait_send()
        behind = gains_ref.at[reach(0, -(k + 1), 1)]
        pltpu.make_async_copy(behind, behind, gain_recv.at[k]).wait()
    most = got_side_ref.at[pl.ds(0, owners - 1)]
    pltpu.make_async_copy(most, most, side_send).wait()
    pltpu.make_async_copy(most, most, side_recv).wait()


def gather_weights(shard, gain, side):
    rows, width = shard.shape
    events = gather_plan()
    hops = sum(kind == "came" for kind, _ in events)
    half = width // 2
    anywhere = pl.BlockSpec(memory_space=pl.ANY)
    dma = pltpu.SemaphoreType.DMA
    return pl.pallas_call(
        functools.partial(gather_kernel, events),
        out_shape=(
            jax.ShapeDtypeStruct((2, *SIZES, 2 * rows, half), shard.dtype),
            jax.ShapeDtypeStruct((SIZES[0], *gain.shape), gain.dtype),
            jax.ShapeDtypeStruct(side.shape, side.dtype),
        ),
        in_specs=[pl.BlockSpec(memory_space=pltpu.VMEM), anywhere, anywhere],
        out_specs=(anywhere, anywhere, anywhere),
        scratch_shapes=[
            pltpu.VMEM((64, half), BF16),
            pltpu.VMEM((64, half), BF16),
            pltpu.VMEM((2 * rows, half), BF16),
            dma,
            dma,
            dma,
            dma,
            dma,
            dma((SIZES[0] - 1,)),
            dma((SIZES[0] - 1,)),
            dma,
            dma,
            dma((hops,)),
            dma((hops,)),
            dma((hops + 1,)),
            dma((hops + 1,)),
        ],
        compiler_params=pltpu.CompilerParams(
            collective_id=0, has_side_effects=True, vmem_limit_bytes=16 << 20
        ),
        name="gather_weights",
    )(shard, gain, side)


def teacher_kernel(
    steps,
    items_ref,
    gains_ref,
    left_ref,
    right_ref,
    student_gain_ref,
    out_gain_ref,
    adapter_ref,
    out_ref,
    total,
    act,
    adapter,
    adapter_sem,
):
    step = pl.program_id(0)
    section = step // steps
    chunk = step % steps
    depth, half = left_ref.shape[2] * left_ref.shape[3], left_ref.shape[4]
    width = 2 * half
    is_value = section % 2 == 0
    is_output = section % 2 == 1
    begins = chunk == 0

    @pl.when(step == 0)
    def _():
        pltpu.make_async_copy(adapter_ref, adapter, adapter_sem).start()
        act[...] = normalize(items_ref[...].astype(F32), gains_ref[0]).astype(BF16)

    @pl.when(begins & (step > 0) & is_value)
    def _():
        hidden = (total[...] * gains_ref[section - 1]).astype(BF16).astype(F32)
        act[...] = normalize(hidden, gains_ref[section]).astype(BF16)

    @pl.when(begins & is_output)
    def _():
        for head in range(width // HD):
            cols = slice(head * HD, (head + 1) * HD)
            values = total[:, cols].astype(BF16).astype(F32)
            scale = lax.rsqrt(jnp.mean(values * values, axis=-1, keepdims=True) + eps)
            act[:, cols] = (values * scale).astype(BF16)

    left = left_ref[0, 0].reshape(depth, half)
    right = right_ref[0, 0].reshape(depth, half)
    place = pl.ds(pl.multiple_of(chunk * depth, HD), depth)

    @pl.when(begins & is_value)
    def _():
        total[:, :half] = dot(act[:, :depth], left)
        total[:, half:width] = dot(act[:, :depth], right)

    @pl.when((chunk > 0) & is_value)
    def _():
        total[:, :half] += dot(act[:, place], left)
        total[:, half:width] += dot(act[:, place], right)

    @pl.when(is_output)
    def _():
        total[:, place] = dot(act[:, :half], left, ((1,), (1,))) + dot(
            act[:, half:width], right, ((1,), (1,))
        )

    @pl.when(step == pl.num_programs(0) - 1)
    def _():
        outcome = (total[...] * gains_ref[section]).astype(BF16).astype(F32)
        act[...] = normalize(outcome, student_gain_ref[...]).astype(BF16)
        pltpu.make_async_copy(adapter_ref, adapter, adapter_sem).wait()
        raw = dot(act[...], adapter[...])
        out_ref[...] = normalize(raw, out_gain_ref[...]).astype(BF16)


def teacher(items, gains, gathered, student_gain, adapter, out_gain):
    rows, width = items.shape
    sections = gathered.shape[1]
    weights = gathered.reshape(2, sections, -1, *gathered.shape[-2:])
    blocks = 16
    steps = weights.shape[2] // blocks
    whole = lambda *shape: pl.BlockSpec(shape, lambda step: (0,) * len(shape))

    def half(part):
        return pl.BlockSpec(
            (1, 1, blocks, *weights.shape[-2:]),
            lambda step: (part, step // steps, step % steps, 0, 0),
        )

    return pl.pallas_call(
        functools.partial(teacher_kernel, steps),
        out_shape=jax.ShapeDtypeStruct((rows, adapter.shape[1]), BF16),
        grid=(sections * steps,),
        in_specs=[
            whole(rows, width),
            whole(sections, 1, width),
            half(0),
            half(1),
            whole(1, width),
            whole(1, adapter.shape[1]),
            pl.BlockSpec(memory_space=pl.ANY),
        ],
        out_specs=whole(rows, adapter.shape[1]),
        scratch_shapes=[
            pltpu.VMEM((rows, width), F32),
            pltpu.VMEM((rows, width), BF16),
            pltpu.VMEM(adapter.shape, BF16),
            pltpu.SemaphoreType.DMA,
        ],
        compiler_params=pltpu.CompilerParams(vmem_limit_bytes=59 << 20),
        name="teacher_chain",
    )(items, gains, weights, weights, student_gain.reshape(1, -1), out_gain.reshape(1, -1), adapter)


def log_softmax(values):
    shifted = values - jnp.max(values, axis=-1, keepdims=True)
    return shifted - jnp.log(jnp.sum(jnp.exp(shifted), axis=-1, keepdims=True))


def pairs_kernel(
    target_ref,
    embed_ref,
    side_ref,
    bank_ref,
    bias_ref,
    neg_ref,
    emb_grad_ref,
    bank_grad_ref,
    kl_ref,
    out_buf,
    got,
    home,
    kl_out,
    kl_home,
    wide,
    slots,
    negatives,
    local_sems,
    send_sem,
    recv_sem,
    back_send,
    back_recv,
    kl_send,
    kl_recv,
):
    me = lax.axis_index("segment") * 64 + lax.axis_index("dp")
    owners, lines, lanes = got.shape
    rows, embed_width = embed_ref.shape
    splits = embed_width // lanes
    picks = target_ref.shape[0]
    capacity = lines // splits
    score_scale = temper * embed_width ** (-0.5)

    barrier = pltpu.get_barrier_semaphore()

    @pl.loop(1, owners)
    def _(i):
        other = (me + i) % owners
        pl.semaphore_signal(barrier, inc=1, device_id=coordinates(other), device_id_type=MESH)

    def send_map(rank):
        slot = lax.broadcasted_iota(jnp.int32, (owners, rows), 0) * capacity + rank
        hit = target_ref[0:1, :] == slot
        for pick in range(1, picks):
            hit = hit | (target_ref[pick : pick + 1, :] == slot)
        return hit.astype(F32).astype(BF16)

    def line(rank, split):
        return pl.ds(rank * splits + split, owners, stride=lines)

    for rank in range(capacity):
        sent = dot(send_map(rank), embed_ref[...])
        for split in range(splits):
            wide[line(rank, split), :] = sent[:, split * lanes : (split + 1) * lanes]
    out_buf[...] = wide[...].reshape(owners, lines, lanes).astype(BF16)

    pl.semaphore_wait(barrier, owners - 1)

    def exchange(src, dst, local, send, recv):
        own = pltpu.make_async_copy(src.at[me], dst.at[me], local)
        own.start()

        @pl.loop(1, owners)
        def _(i):
            other = (me + i) % owners
            pltpu.make_async_remote_copy(
                src_ref=src.at[other],
                dst_ref=dst.at[me],
                send_sem=send,
                recv_sem=recv,
                device_id=coordinates(other),
                device_id_type=MESH,
            ).start()

        return own

    def finish(dst, own, send, recv):
        own.wait()
        most = dst.at[pl.ds(0, owners - 1)]
        pltpu.make_async_copy(most, most, recv).wait()
        pltpu.make_async_copy(most, most, send).wait()

    own = exchange(out_buf, got, local_sems.at[0], send_sem, recv_sem)

    pool = bank_ref.shape[0]
    negs = neg_ref.shape[1]
    chosen = neg_ref[...] == lax.broadcasted_iota(jnp.int32, (pool, negs), 0)
    choose = chosen.astype(F32).astype(BF16)
    negatives[...] = dot(choose, bank_ref[...], ((0,), (0,))).astype(BF16)
    offsets = jnp.sum(jnp.where(chosen, bias_ref[...], 0.0), axis=0, keepdims=True)
    valid = (side_ref[:, 0:1] > 0.5 * UNUSED).astype(F32)
    teacher_log = log_softmax(side_ref[...])
    teacher_prob = jnp.exp(teacher_log)

    finish(got, own, send_sem, recv_sem)
    wide[...] = got[...].astype(F32).reshape(owners * lines, lanes)
    for rank in range(capacity):
        for split in range(splits):
            slots[rank * owners : (rank + 1) * owners, split * lanes : (split + 1) * lanes] = wide[
                line(rank, split), :
            ].astype(BF16)

    logits = dot(slots[...], negatives[...], ((1,), (1,))) * score_scale + offsets
    student_log = log_softmax(logits)
    divergence = jnp.sum(teacher_prob * (teacher_log - student_log), axis=-1, keepdims=True)
    divergence = divergence.astype(BF16).astype(F32)
    lane = lax.broadcasted_iota(jnp.int32, (owners, lanes), 1)
    spread = jnp.zeros((owners, lanes), F32)
    for rank in range(capacity):
        spread = jnp.where(lane == rank, divergence[rank * owners : (rank + 1) * owners], spread)
    kl_out[...] = spread.reshape(owners, 1, lanes)

    gap = (valid * (jnp.exp(student_log) - teacher_prob)).astype(BF16)
    for rank in range(capacity):
        grad = dot(gap[rank * owners : (rank + 1) * owners], negatives[...]) * score_scale
        for split in range(splits):
            wide[line(rank, split), :] = grad[:, split * lanes : (split + 1) * lanes]
    out_buf[...] = wide[...].reshape(owners, lines, lanes).astype(BF16)
    own = exchange(out_buf, home, local_sems.at[2], back_send, back_recv)
    kl_own = exchange(kl_out, kl_home, local_sems.at[1], kl_send, kl_recv)

    rest = dot(gap, slots[...], ((0,), (0,))) * score_scale
    bank_grad = jnp.zeros(bank_grad_ref.shape, F32)
    for _ in range(3):
        term = rest.astype(BF16)
        bank_grad = bank_grad + dot(choose, term)
        rest = rest - term.astype(F32)
    bank_grad_ref[...] = bank_grad

    finish(kl_home, kl_own, kl_send, kl_recv)
    kl_ref[...] = kl_home[...].reshape(owners, lanes)
    finish(home, own, back_send, back_recv)
    wide[...] = home[...].astype(F32).reshape(owners * lines, lanes)
    for rank in range(capacity):
        for split in range(splits):
            slots[rank * owners : (rank + 1) * owners, split * lanes : (split + 1) * lanes] = wide[
                line(rank, split), :
            ].astype(BF16)
    emb_grad = jnp.zeros(emb_grad_ref.shape, F32)
    for rank in range(capacity):
        held = slots[rank * owners : (rank + 1) * owners, :]
        emb_grad = emb_grad + dot(send_map(rank), held, ((0,), (0,)))
    emb_grad_ref[...] = emb_grad


def pairs(target, embedding, side, bank, bank_bias, neg_index, owners, capacity):
    rows, embed_width = embedding.shape
    lines = capacity * embed_width // HD
    vmem = pl.BlockSpec(memory_space=pltpu.VMEM)
    dma = pltpu.SemaphoreType.DMA
    return pl.pallas_call(
        pairs_kernel,
        out_shape=(
            jax.ShapeDtypeStruct((rows, embed_width), F32),
            jax.ShapeDtypeStruct(bank.shape, F32),
            jax.ShapeDtypeStruct((owners, HD), F32),
        ),
        in_specs=[vmem] * 6,
        out_specs=(vmem,) * 3,
        scratch_shapes=[
            pltpu.VMEM((owners, lines, HD), BF16),
            pltpu.VMEM((owners, lines, HD), BF16),
            pltpu.VMEM((owners, lines, HD), BF16),
            pltpu.VMEM((owners, 1, HD), F32),
            pltpu.VMEM((owners, 1, HD), F32),
            pltpu.VMEM((owners * lines, HD), F32),
            pltpu.VMEM((owners * capacity, embed_width), BF16),
            pltpu.VMEM((neg_index.shape[1], embed_width), BF16),
            dma((3,)),
            dma,
            dma,
            dma,
            dma,
            dma,
            dma,
        ],
        compiler_params=pltpu.CompilerParams(
            collective_id=1, has_side_effects=True, vmem_limit_bytes=40 << 20
        ),
        name="pair_exchange",
    )(target, embedding, side, bank, bank_bias.reshape(-1, 1), neg_index)


def shards(
    items,
    section_weights,
    section_gains,
    student_gain,
    adapter,
    out_gain,
    assign,
    teacher_scores,
    bank,
    bank_bias,
    neg_index,
):
    owners = lax.axis_size("segment") * lax.axis_size("dp")
    row_count, pick_count = assign.shape
    pair_count = row_count * pick_count
    capacity = 2
    slot_count = owners * capacity

    pair_cluster = assign.reshape(-1)
    same = pair_cluster[:, None] == pair_cluster[None, :]
    earlier = jnp.arange(pair_count)[:, None] > jnp.arange(pair_count)[None, :]
    pair_rank = jnp.sum((same & earlier).astype(jnp.int32), axis=1)
    target = pair_cluster * capacity + pair_rank
    pick_map = target[None, :] == jnp.arange(slot_count, dtype=jnp.int32)[:, None]
    scores = teacher_scores.reshape(pair_count, -1)
    side = jnp.dot(pick_map.astype(BF16), scores, preferred_element_type=F32)
    side = jnp.where(jnp.any(pick_map, axis=1, keepdims=True), side, UNUSED)
    side = side.reshape(owners, capacity, -1)

    gathered, gains, got_side = gather_weights(
        section_weights[0], section_gains.reshape(1, -1), side
    )
    embedding = teacher(items, gains, gathered, student_gain, adapter, out_gain)
    slot_side = got_side.transpose(1, 0, 2).reshape(slot_count, -1)
    target_rows = target.reshape(row_count, pick_count).T
    emb_grad, bank_grad, owner_kl = pairs(
        target_rows, embedding, slot_side, bank, bank_bias, neg_index, owners, capacity
    )
    slot_kl = owner_kl[:, :capacity].reshape(slot_count)
    row_kl = jnp.sum(jnp.where(pick_map, slot_kl[:, None], 0.0), axis=0)
    row_kl = row_kl.astype(BF16).reshape(row_count, pick_count)
    return (emb_grad, row_kl, bank_grad)


def solution(mesh):
    in_specs = (
        P(("segment", "dp"), None),
        P("segment", "dp", None),
        P("segment", None),
        P(),
        P(),
        P(),
        P(("segment", "dp"), None),
        P(("segment", "dp"), None, None),
        P(("segment", "dp"), None),
        P(("segment", "dp")),
        P(("segment", "dp"), None),
    )
    out_specs = (P(("segment", "dp"), None), P(("segment", "dp"), None), P(("segment", "dp"), None))
    return jax.shard_map(shards, mesh=mesh, in_specs=in_specs, out_specs=out_specs, check_vma=False)
```

```python
import functools

import jax
import jax.numpy as jnp
from jax import lax
from jax.experimental import pallas as pl
from jax.experimental.pallas import tpu as pltpu
from jax.sharding import PartitionSpec as P

HD = 128
MESH = pl.DeviceIdType.MESH
F32 = jnp.float32
BF16 = jnp.bfloat16

eps = 1e-06
temper = 4.0
UNUSED = -1e30

SIZES = (4, 4, 8)
ORDERS = ((0, 1, 2), (2, 1, 0), (0, 2, 1))
PART_ROWS = (32, 48, 32)
GROUPED = (True, False, False)


def dot(a, b, contract=((1,), (0,))):
    return lax.dot_general(a, b, (contract, ((), ())), preferred_element_type=F32)


def normalize(values, scale_row):
    return values * lax.rsqrt(jnp.mean(values * values, axis=-1, keepdims=True) + eps) * scale_row


def offsets_along(size):
    return [0] + list(range(1, size // 2 + 1)) + [-k for k in range(1, size // 2)]


def gather_plan(window=8, latency=140.0, release=60.0):
    rows, needs = {}, {}
    for part, order in enumerate(ORDERS):
        for phase, axis in enumerate(order):
            if phase == 0:
                subs = [()]
            elif phase == 1:
                subs = [(k,) for k in offsets_along(SIZES[order[0]])]
            else:
                firsts = [None] if GROUPED[part] else offsets_along(SIZES[order[0]])
                subs = [(j, k) for j in firsts for k in offsets_along(SIZES[order[1]])]
            for sub in subs:
                count = PART_ROWS[part] * (SIZES[order[0]] if None in sub else 1)
                for k in offsets_along(SIZES[axis]):
                    if k:
                        rows[part, phase, k, sub] = count

    def waits_for(hop):
        part, phase, k, sub = hop
        if abs(k) > 1:
            return [(part, phase, k - 1 if k > 0 else k + 1, sub)]
        if phase == 0:
            return []
        if phase == 1:
            return [(part, 0, sub[0], ())] if sub[0] else []
        found = []
        for j in offsets_along(SIZES[ORDERS[part][0]]) if sub[0] is None else [sub[0]]:
            if sub[1]:
                found.append((part, 1, sub[1], (j,)))
            elif j:
                found.append((part, 0, j, ()))
        return found

    for hop in rows:
        needs[hop] = waits_for(hop)

    def axis_of(hop):
        return ORDERS[hop[0]][hop[1]]

    def lane_of(hop):
        return (axis_of(hop), hop[2] > 0)

    def urgency(hop):
        size = SIZES[axis_of(hop)]
        rest = size // 2 - hop[2] if hop[2] > 0 else size // 2 - 1 + hop[2]
        return (hop[1], -rest, str(hop))

    queues = {(axis, long_way): [] for axis in range(3) for long_way in (True, False)}
    flying = dict.fromkeys(queues, 0)
    for hop in rows:
        if not needs[hop]:
            queues[lane_of(hop)].append(hop)
    events, active, landing, leaving, came = [], {}, {}, {}, set()
    now = 0.0
    while True:
        for lane, queue in queues.items():
            while queue and flying[lane] < window:
                queue.sort(key=urgency)
                hop = queue.pop(0)
                active[hop] = float(rows[hop])
                flying[lane] += 1
                events.append((round(now, 3), 2, str(hop), "start", hop))
        if not (active or landing or leaving):
            break
        load = [0, 0, 0]
        for hop in active:
            load[axis_of(hop)] += 1
        step = min(
            [left * load[axis_of(hop)] for hop, left in active.items()]
            + [end - now for end in landing.values()]
            + [end - now for end in leaving.values()]
        )
        now += step
        for hop in list(active):
            active[hop] -= step / load[axis_of(hop)]
            if active[hop] < 1e-6:
                del active[hop]
                landing[hop] = now + latency
                leaving[hop] = now + release
        for hop in [h for h, end in leaving.items() if end <= now + 1e-6]:
            del leaving[hop]
            flying[lane_of(hop)] -= 1
            events.append((round(now, 3), 1, str(hop), "sent", hop))
        for hop in [h for h, end in landing.items() if end <= now + 1e-6]:
            del landing[hop]
            came.add(hop)
            events.append((round(now, 3), 0, str(hop), "came", hop))
            for user in rows:
                if hop in needs[user] and all(d in came for d in needs[user]):
                    queues[lane_of(user)].append(user)
    begun = {(lane_of(hop), at) for at, _, _, kind, hop in events if kind == "start"}
    return [
        (kind, hop)
        for at, _, _, kind, hop in sorted(events, key=lambda event: event[:3])
        if kind != "sent" or (lane_of(hop), at) in begun
    ]


def coordinates(index):
    return (index // 64, index % 64)


def gather_kernel(
    events,
    shard_ref,
    gain_ref,
    side_ref,
    out_ref,
    gains_ref,
    got_side_ref,
    away,
    came,
    block,
    local_sem,
    gain_local,
    side_local,
    pair_send,
    pair_recv,
    gain_send,
    gain_recv,
    side_send,
    side_recv,
    send_sem,
    recv_sem,
    sib_send,
    sib_recv,
):
    x = lax.axis_index("segment")
    dp = lax.axis_index("dp")
    me = x * 64 + dp
    core = dp % 2
    z = (dp // 2) % SIZES[2]
    y = dp // (2 * SIZES[2])
    here = (x, y, z)
    sign = 1 - 2 * core
    owners = side_ref.shape[0]

    barrier = pltpu.get_barrier_semaphore()

    @pl.loop(1, owners)
    def _(i):
        other = (me + i) % owners
        pl.semaphore_signal(barrier, inc=1, device_id=coordinates(other), device_id_type=MESH)

    rows, width = shard_ref.shape
    half = width // 2
    keep = shard_ref[:, pl.ds(pl.multiple_of(core * half, HD), half)].astype(F32)
    other_half = shard_ref[:, pl.ds(pl.multiple_of((1 - core) * half, HD), half)].astype(F32)
    spare = jnp.zeros((away.shape[0] - rows, half), F32)
    away[...] = jnp.concatenate([other_half, spare], axis=0).astype(BF16)
    gain_copy = pltpu.make_async_copy(gain_ref, gains_ref.at[x], gain_local)
    gain_copy.start()
    side_copy = pltpu.make_async_copy(side_ref.at[me], got_side_ref.at[me], side_local)
    side_copy.start()

    pl.semaphore_wait(barrier, owners - 1)

    def device(at, on):
        return (at[0], (at[1] * SIZES[2] + at[2]) * 2 + on)

    def reach(axis, k, way):
        return (here[axis] + way * k + 2 * SIZES[axis]) % SIZES[axis]

    sibling = device(here, 1 - core)
    pair = pltpu.make_async_remote_copy(
        src_ref=away,
        dst_ref=came,
        send_sem=pair_send,
        recv_sem=pair_recv,
        device_id=sibling,
        device_id_type=MESH,
    )
    pair.start()
    gain_copies = []
    for k in range(1, SIZES[0]):
        copy = pltpu.make_async_remote_copy(
            src_ref=gain_ref,
            dst_ref=gains_ref.at[x],
            send_sem=gain_send.at[k - 1],
            recv_sem=gain_recv.at[k - 1],
            device_id=(reach(0, k, 1), dp),
            device_id_type=MESH,
        )
        copy.start()
        gain_copies.append(copy)
    pair.wait_recv()
    theirs = came[...].astype(F32)[:rows]

    @pl.when(core == 0)
    def _():
        block[...] = jnp.concatenate([keep, theirs], axis=0).astype(BF16)

    @pl.when(core == 1)
    def _():
        block[...] = jnp.concatenate([theirs, keep], axis=0).astype(BF16)

    mine = pltpu.make_async_copy(block, out_ref.at[core, x, y, z], local_sem)
    mine.start()

    starts = [sum(PART_ROWS[:part]) for part in range(len(PART_ROWS))]
    plan = [hop for kind, hop in events if kind == "came"]
    number = {hop: i for i, hop in enumerate(plan)}

    def held(hop, travelled, on, way):
        part, phase, _, sub = hop
        order = ORDERS[part]
        at = list(here)
        at[order[phase]] = reach(order[phase], -travelled, way)
        for axis, k in zip(order[:phase], sub):
            at[axis] = slice(None) if k is None else reach(axis, -k, way)
        return out_ref.at[
            on, at[0], at[1], at[2], pl.ds(starts[part], PART_ROWS[part]), :
        ]

    def hop_copy(hop, sending):
        part, phase, k, _ = hop
        axis = ORDERS[part][phase]
        step = 1 if k > 0 else -1
        ref = held(hop, k - step if sending else k, core, sign)
        to = list(here)
        to[axis] = reach(axis, step, sign)
        fresh = sending and k == step and not any(j is None or j for j in hop[3])
        rows_of = pl.ds(starts[part], PART_ROWS[part])
        return pltpu.make_async_remote_copy(
            src_ref=block.at[rows_of, :] if fresh else ref,
            dst_ref=ref,
            send_sem=send_sem.at[number[hop]],
            recv_sem=recv_sem.at[number[hop]],
            device_id=device(to, core),
            device_id_type=MESH,
        )

    def share(hop, on, way):
        ref = out_ref.at[on, x, y, z] if hop is None else held(hop, hop[2], on, way)
        index = len(plan) if hop is None else number[hop]
        return pltpu.make_async_remote_copy(
            src_ref=block if hop is None else ref,
            dst_ref=ref,
            send_sem=sib_send.at[index],
            recv_sem=sib_recv.at[index],
            device_id=sibling,
            device_id_type=MESH,
        )

    def send_side(begin, end):
        @pl.loop(begin, end)
        def _(i):
            other = (me + i) % owners
            pltpu.make_async_remote_copy(
                src_ref=side_ref.at[other],
                dst_ref=got_side_ref.at[me],
                send_sem=side_send,
                recv_sem=side_recv,
                device_id=coordinates(other),
                device_id_type=MESH,
            ).start()

    shares = [share(None, core, sign)]
    shares[0].start()
    copies = {}
    pieces = [(begin, min(begin + 32, owners)) for begin in range(1, owners, 32)]
    newest = []

    def pass_on():
        for hop in newest:
            shares.append(share(hop, core, sign))
            shares[-1].start()
            if len(shares) > 60 and len(shares) % 16 == 0 and pieces:
                send_side(*pieces.pop(0))
        newest.clear()

    for kind, hop in events:
        if kind == "start":
            copies[hop] = hop_copy(hop, True)
            copies[hop].start()
        elif kind == "sent":
            copies.pop(hop).wait_send()
        else:
            pass_on()
            if hop == plan[0]:
                mine.wait()
            hop_copy(hop, False).wait_recv()
            newest.append(hop)

    pass_on()
    for hop in [None] + plan:
        share(hop, 1 - core, -sign).wait_recv()
    for copy in shares + list(copies.values()):
        copy.wait_send()
    pair.wait_send()
    gain_copy.wait()
    side_copy.wait()
    for k, copy in enumerate(gain_copies):
        copy.wait_send()
        behind = gains_ref.at[reach(0, -(k + 1), 1)]
        pltpu.make_async_copy(behind, behind, gain_recv.at[k]).wait()
    most = got_side_ref.at[pl.ds(0, owners - 1)]
    pltpu.make_async_copy(most, most, side_send).wait()
    pltpu.make_async_copy(most, most, side_recv).wait()


def gather_weights(shard, gain, side):
    rows, width = shard.shape
    events = gather_plan()
    hops = sum(kind == "came" for kind, _ in events)
    half = width // 2
    anywhere = pl.BlockSpec(memory_space=pl.ANY)
    dma = pltpu.SemaphoreType.DMA
    return pl.pallas_call(
        functools.partial(gather_kernel, events),
        out_shape=(
            jax.ShapeDtypeStruct((2, *SIZES, 2 * rows, half), shard.dtype),
            jax.ShapeDtypeStruct((SIZES[0], *gain.shape), gain.dtype),
            jax.ShapeDtypeStruct(side.shape, side.dtype),
        ),
        in_specs=[pl.BlockSpec(memory_space=pltpu.VMEM), anywhere, anywhere],
        out_specs=(anywhere, anywhere, anywhere),
        scratch_shapes=[
            pltpu.VMEM((64, half), BF16),
            pltpu.VMEM((64, half), BF16),
            pltpu.VMEM((2 * rows, half), BF16),
            dma,
            dma,
            dma,
            dma,
            dma,
            dma((SIZES[0] - 1,)),
            dma((SIZES[0] - 1,)),
            dma,
            dma,
            dma((hops,)),
            dma((hops,)),
            dma((hops + 1,)),
            dma((hops + 1,)),
        ],
        compiler_params=pltpu.CompilerParams(
            collective_id=0, has_side_effects=True, vmem_limit_bytes=16 << 20
        ),
        name="gather_weights",
    )(shard, gain, side)


def teacher_kernel(
    steps,
    items_ref,
    gains_ref,
    left_ref,
    right_ref,
    student_gain_ref,
    out_gain_ref,
    adapter_ref,
    out_ref,
    total,
    act,
    adapter,
    adapter_sem,
):
    step = pl.program_id(0)
    section = step // steps
    chunk = step % steps
    depth, half = left_ref.shape[2] * left_ref.shape[3], left_ref.shape[4]
    width = 2 * half
    is_value = section % 2 == 0
    is_output = section % 2 == 1
    begins = chunk == 0

    @pl.when(step == 0)
    def _():
        pltpu.make_async_copy(adapter_ref, adapter, adapter_sem).start()
        act[...] = normalize(items_ref[...].astype(F32), gains_ref[0]).astype(BF16)

    @pl.when(begins & (step > 0) & is_value)
    def _():
        hidden = (total[...] * gains_ref[section - 1]).astype(BF16).astype(F32)
        act[...] = normalize(hidden, gains_ref[section]).astype(BF16)

    @pl.when(begins & is_output)
    def _():
        for head in range(width // HD):
            cols = slice(head * HD, (head + 1) * HD)
            values = total[:, cols].astype(BF16).astype(F32)
            scale = lax.rsqrt(jnp.mean(values * values, axis=-1, keepdims=True) + eps)
            act[:, cols] = (values * scale).astype(BF16)

    left = left_ref[0, 0].reshape(depth, half)
    right = right_ref[0, 0].reshape(depth, half)
    place = pl.ds(pl.multiple_of(chunk * depth, HD), depth)

    cut = half // 256 * 256
    seam = 2 * (half - cut)
    middle = jnp.concatenate([left[:, cut:], right[:, : half - cut]], axis=1)
    pieces = (
        (slice(0, cut), left[:, :cut]),
        (slice(cut, cut + seam), middle),
        (slice(cut + seam, width), right[:, half - cut :]),
    )

    @pl.when(begins & is_value)
    def _():
        for cols, piece in pieces:
            total[:, cols] = dot(act[:, :depth], piece)

    @pl.when((chunk > 0) & is_value)
    def _():
        for cols, piece in pieces:
            total[:, cols] += dot(act[:, place], piece)

    @pl.when(is_output)
    def _():
        parts = [dot(act[:, cols], piece, ((1,), (1,))) for cols, piece in pieces]
        total[:, place] = parts[0] + parts[1] + parts[2]

    @pl.when(step == pl.num_programs(0) - 1)
    def _():
        outcome = (total[...] * gains_ref[section]).astype(BF16).astype(F32)
        act[...] = normalize(outcome, student_gain_ref[...]).astype(BF16)
        pltpu.make_async_copy(adapter_ref, adapter, adapter_sem).wait()
        raw = dot(act[...], adapter[...])
        out_ref[...] = normalize(raw, out_gain_ref[...]).astype(BF16)


def teacher(items, gains, gathered, student_gain, adapter, out_gain):
    rows, width = items.shape
    sections = gathered.shape[1]
    weights = gathered.reshape(2, sections, -1, *gathered.shape[-2:])
    blocks = 16
    steps = weights.shape[2] // blocks
    whole = lambda *shape: pl.BlockSpec(shape, lambda step: (0,) * len(shape))

    def half(part):
        return pl.BlockSpec(
            (1, 1, blocks, *weights.shape[-2:]),
            lambda step: (part, step // steps, step % steps, 0, 0),
        )

    return pl.pallas_call(
        functools.partial(teacher_kernel, steps),
        out_shape=jax.ShapeDtypeStruct((rows, adapter.shape[1]), BF16),
        grid=(sections * steps,),
        in_specs=[
            whole(rows, width),
            whole(sections, 1, width),
            half(0),
            half(1),
            whole(1, width),
            whole(1, adapter.shape[1]),
            pl.BlockSpec(memory_space=pl.ANY),
        ],
        out_specs=whole(rows, adapter.shape[1]),
        scratch_shapes=[
            pltpu.VMEM((rows, width), F32),
            pltpu.VMEM((rows, width), BF16),
            pltpu.VMEM(adapter.shape, BF16),
            pltpu.SemaphoreType.DMA,
        ],
        compiler_params=pltpu.CompilerParams(vmem_limit_bytes=59 << 20),
        name="teacher_chain",
    )(items, gains, weights, weights, student_gain.reshape(1, -1), out_gain.reshape(1, -1), adapter)


def log_softmax(values):
    shifted = values - jnp.max(values, axis=-1, keepdims=True)
    return shifted - jnp.log(jnp.sum(jnp.exp(shifted), axis=-1, keepdims=True))


def pairs_kernel(
    target_ref,
    embed_ref,
    side_ref,
    bank_ref,
    bias_ref,
    neg_ref,
    emb_grad_ref,
    bank_grad_ref,
    kl_ref,
    out_buf,
    got,
    home,
    kl_out,
    kl_home,
    wide,
    slots,
    negatives,
    local_sems,
    send_sem,
    recv_sem,
    back_send,
    back_recv,
    kl_send,
    kl_recv,
):
    me = lax.axis_index("segment") * 64 + lax.axis_index("dp")
    owners, lines, lanes = got.shape
    rows, embed_width = embed_ref.shape
    splits = embed_width // lanes
    picks = target_ref.shape[0]
    capacity = lines // splits
    score_scale = temper * embed_width ** (-0.5)

    barrier = pltpu.get_barrier_semaphore()

    @pl.loop(1, owners)
    def _(i):
        other = (me + i) % owners
        pl.semaphore_signal(barrier, inc=1, device_id=coordinates(other), device_id_type=MESH)

    def send_map(rank):
        slot = lax.broadcasted_iota(jnp.int32, (owners, rows), 0) * capacity + rank
        hit = target_ref[0:1, :] == slot
        for pick in range(1, picks):
            hit = hit | (target_ref[pick : pick + 1, :] == slot)
        return hit.astype(F32).astype(BF16)

    def line(rank, split):
        return pl.ds(rank * splits + split, owners, stride=lines)

    for rank in range(capacity):
        sent = dot(send_map(rank), embed_ref[...])
        for split in range(splits):
            wide[line(rank, split), :] = sent[:, split * lanes : (split + 1) * lanes]
    out_buf[...] = wide[...].reshape(owners, lines, lanes).astype(BF16)

    pl.semaphore_wait(barrier, owners - 1)

    def exchange(src, dst, local, send, recv):
        own = pltpu.make_async_copy(src.at[me], dst.at[me], local)
        own.start()

        @pl.loop(1, owners)
        def _(i):
            other = (me + i) % owners
            pltpu.make_async_remote_copy(
                src_ref=src.at[other],
                dst_ref=dst.at[me],
                send_sem=send,
                recv_sem=recv,
                device_id=coordinates(other),
                device_id_type=MESH,
            ).start()

        return own

    def finish(dst, own, send, recv):
        own.wait()
        most = dst.at[pl.ds(0, owners - 1)]
        pltpu.make_async_copy(most, most, recv).wait()
        pltpu.make_async_copy(most, most, send).wait()

    own = exchange(out_buf, got, local_sems.at[0], send_sem, recv_sem)

    pool = bank_ref.shape[0]
    negs = neg_ref.shape[1]
    chosen = neg_ref[...] == lax.broadcasted_iota(jnp.int32, (pool, negs), 0)
    choose = chosen.astype(F32).astype(BF16)
    negatives[...] = dot(choose, bank_ref[...], ((0,), (0,))).astype(BF16)
    offsets = jnp.sum(jnp.where(chosen, bias_ref[...], 0.0), axis=0, keepdims=True)
    valid = (side_ref[:, 0:1] > 0.5 * UNUSED).astype(F32)
    teacher_log = log_softmax(side_ref[...])
    teacher_prob = jnp.exp(teacher_log)

    finish(got, own, send_sem, recv_sem)
    wide[...] = got[...].astype(F32).reshape(owners * lines, lanes)
    for rank in range(capacity):
        for split in range(splits):
            slots[rank * owners : (rank + 1) * owners, split * lanes : (split + 1) * lanes] = wide[
                line(rank, split), :
            ].astype(BF16)

    logits = dot(slots[...], negatives[...], ((1,), (1,))) * score_scale + offsets
    student_log = log_softmax(logits)
    divergence = jnp.sum(teacher_prob * (teacher_log - student_log), axis=-1, keepdims=True)
    divergence = divergence.astype(BF16).astype(F32)
    lane = lax.broadcasted_iota(jnp.int32, (owners, lanes), 1)
    spread = jnp.zeros((owners, lanes), F32)
    for rank in range(capacity):
        spread = jnp.where(lane == rank, divergence[rank * owners : (rank + 1) * owners], spread)
    kl_out[...] = spread.reshape(owners, 1, lanes)

    gap = (valid * (jnp.exp(student_log) - teacher_prob)).astype(BF16)
    for rank in range(capacity):
        grad = dot(gap[rank * owners : (rank + 1) * owners], negatives[...]) * score_scale
        for split in range(splits):
            wide[line(rank, split), :] = grad[:, split * lanes : (split + 1) * lanes]
    out_buf[...] = wide[...].reshape(owners, lines, lanes).astype(BF16)
    own = exchange(out_buf, home, local_sems.at[2], back_send, back_recv)
    kl_own = exchange(kl_out, kl_home, local_sems.at[1], kl_send, kl_recv)

    rest = dot(gap, slots[...], ((0,), (0,))) * score_scale
    bank_grad = jnp.zeros(bank_grad_ref.shape, F32)
    for _ in range(3):
        term = rest.astype(BF16)
        bank_grad = bank_grad + dot(choose, term)
        rest = rest - term.astype(F32)
    bank_grad_ref[...] = bank_grad

    finish(kl_home, kl_own, kl_send, kl_recv)
    kl_ref[...] = kl_home[...].reshape(owners, lanes)
    finish(home, own, back_send, back_recv)
    wide[...] = home[...].astype(F32).reshape(owners * lines, lanes)
    for rank in range(capacity):
        for split in range(splits):
            slots[rank * owners : (rank + 1) * owners, split * lanes : (split + 1) * lanes] = wide[
                line(rank, split), :
            ].astype(BF16)
    emb_grad = jnp.zeros(emb_grad_ref.shape, F32)
    for rank in range(capacity):
        held = slots[rank * owners : (rank + 1) * owners, :]
        emb_grad = emb_grad + dot(send_map(rank), held, ((0,), (0,)))
    emb_grad_ref[...] = emb_grad


def pairs(target, embedding, side, bank, bank_bias, neg_index, owners, capacity):
    rows, embed_width = embedding.shape
    lines = capacity * embed_width // HD
    vmem = pl.BlockSpec(memory_space=pltpu.VMEM)
    dma = pltpu.SemaphoreType.DMA
    return pl.pallas_call(
        pairs_kernel,
        out_shape=(
            jax.ShapeDtypeStruct((rows, embed_width), F32),
            jax.ShapeDtypeStruct(bank.shape, F32),
            jax.ShapeDtypeStruct((owners, HD), F32),
        ),
        in_specs=[vmem] * 6,
        out_specs=(vmem,) * 3,
        scratch_shapes=[
            pltpu.VMEM((owners, lines, HD), BF16),
            pltpu.VMEM((owners, lines, HD), BF16),
            pltpu.VMEM((owners, lines, HD), BF16),
            pltpu.VMEM((owners, 1, HD), F32),
            pltpu.VMEM((owners, 1, HD), F32),
            pltpu.VMEM((owners * lines, HD), F32),
            pltpu.VMEM((owners * capacity, embed_width), BF16),
            pltpu.VMEM((neg_index.shape[1], embed_width), BF16),
            dma((3,)),
            dma,
            dma,
            dma,
            dma,
            dma,
            dma,
        ],
        compiler_params=pltpu.CompilerParams(
            collective_id=1, has_side_effects=True, vmem_limit_bytes=40 << 20
        ),
        name="pair_exchange",
    )(target, embedding, side, bank, bank_bias.reshape(-1, 1), neg_index)


def shards(
    items,
    section_weights,
    section_gains,
    student_gain,
    adapter,
    out_gain,
    assign,
    teacher_scores,
    bank,
    bank_bias,
    neg_index,
):
    owners = lax.axis_size("segment") * lax.axis_size("dp")
    row_count, pick_count = assign.shape
    pair_count = row_count * pick_count
    capacity = 2
    slot_count = owners * capacity

    pair_cluster = assign.reshape(-1)
    same = pair_cluster[:, None] == pair_cluster[None, :]
    earlier = jnp.arange(pair_count)[:, None] > jnp.arange(pair_count)[None, :]
    pair_rank = jnp.sum((same & earlier).astype(jnp.int32), axis=1)
    target = pair_cluster * capacity + pair_rank
    pick_map = target[None, :] == jnp.arange(slot_count, dtype=jnp.int32)[:, None]
    scores = teacher_scores.reshape(pair_count, -1)
    side = jnp.dot(pick_map.astype(BF16), scores, preferred_element_type=F32)
    side = jnp.where(jnp.any(pick_map, axis=1, keepdims=True), side, UNUSED)
    side = side.reshape(owners, capacity, -1)

    gathered, gains, got_side = gather_weights(
        section_weights[0], section_gains.reshape(1, -1), side
    )
    embedding = teacher(items, gains, gathered, student_gain, adapter, out_gain)
    slot_side = got_side.transpose(1, 0, 2).reshape(slot_count, -1)
    target_rows = target.reshape(row_count, pick_count).T
    emb_grad, bank_grad, owner_kl = pairs(
        target_rows, embedding, slot_side, bank, bank_bias, neg_index, owners, capacity
    )
    slot_kl = owner_kl[:, :capacity].reshape(slot_count)
    row_kl = jnp.sum(jnp.where(pick_map, slot_kl[:, None], 0.0), axis=0)
    row_kl = row_kl.astype(BF16).reshape(row_count, pick_count)
    return (emb_grad, row_kl, bank_grad)


def solution(mesh):
    in_specs = (
        P(("segment", "dp"), None),
        P("segment", "dp", None),
        P("segment", None),
        P(),
        P(),
        P(),
        P(("segment", "dp"), None),
        P(("segment", "dp"), None, None),
        P(("segment", "dp"), None),
        P(("segment", "dp")),
        P(("segment", "dp"), None),
    )
    out_specs = (P(("segment", "dp"), None), P(("segment", "dp"), None), P(("segment", "dp"), None))
    return jax.shard_map(shards, mesh=mesh, in_specs=in_specs, out_specs=out_specs, check_vma=False)
```
